32 devices in a mesh: section: 2 (over core), fsdp: 16 (over z, y, x).
Axes of the slice: x: 2, y: 2, z: 4, core: 2. Of those that a mesh axis runs over, the one named last changes fastest.
Arguments:
- inputs: bfloat16 [2, 6144, 960], P(None, 'fsdp'), may hold values from -6 to 6
- cotangent: float32 [2, 6144, 960], P(None, 'fsdp'), may hold values from -6 to 6
- segments: int32 [2, 6144], P(None, 'fsdp'), may hold values from 0 to 2, as said below
- positions: int32 [2, 6144], P(None, 'fsdp'), may hold values from 0 to 2430, as said below
- norm_first: bfloat16 [2, 960], P('section', 'fsdp'), may hold values from 0.099609375 to 1.8984375
- w_query: bfloat16 [2, 960, 960], P('section', 'fsdp'), may hold values from -0.1875 to 0.1875
- w_key: bfloat16 [2, 960, 320], P('section', 'fsdp'), may hold values from -0.1875 to 0.1875
- w_value: bfloat16 [2, 960, 320], P('section', 'fsdp'), may hold values from -0.1875 to 0.1875
- w_out: bfloat16 [2, 960, 960], P('section', 'fsdp'), may hold values from -0.5 to 0.5
- norm_second: bfloat16 [2, 960], P('section', 'fsdp'), may hold values from 0.099609375 to 1.8984375
- w_gate: bfloat16 [2, 960, 2560], P('section', 'fsdp'), may hold values from -0.1875 to 0.1875
- w_up: bfloat16 [2, 960, 2560], P('section', 'fsdp'), may hold values from -0.1875 to 0.1875
- w_down: bfloat16 [2, 2560, 960], P('section', 'fsdp'), may hold values from -0.125 to 0.125
Outputs:
- activations: float32 [2, 2, 6144, 960], P('section', None, 'fsdp')
- input_grads: float32 [2, 2, 6144, 960], P('section', None, 'fsdp')
- grad_norm_first: float32 [2, 960], P('section', 'fsdp')
- grad_query: float32 [2, 960, 960], P('section', 'fsdp')
- grad_key: float32 [2, 960, 320], P('section', 'fsdp')
- grad_value: float32 [2, 960, 320], P('section', 'fsdp')
- grad_out: float32 [2, 960, 960], P('section', 'fsdp')
- grad_norm_second: float32 [2, 960], P('section', 'fsdp')
- grad_gate: float32 [2, 960, 2560], P('section', 'fsdp')
- grad_up: float32 [2, 960, 2560], P('section', 'fsdp')
- grad_down: float32 [2, 2560, 960], P('section', 'fsdp')
The draws below stay inside these ranges and needn't reach their ends.
Inputs may be any that keep to these rules, and one draw needn't show every extreme that they name: `segments`: each sequence of 384 tokens holds exactly three documents, numbered 0, 1, 2 in order; a document is a run of equal numbers. Within a document positions rise by one from token to token from a start below 2048.
All inputs are finite; a program needn't handle non-finite values.
Results may differ from the reference program's by a relative error of at most 0.025.
Values may be sent and summed in bfloat16 or wider, within the bound.
No kernel may reach another device: no remote copies, remote signals or barrier semaphores. Data moves between devices by JAX's collectives and lax.ppermute only.
A program may use at most 320 MiB of HBM per device.

```python
import jax
import jax.numpy as jnp
from jax import lax

D = 960
HEADS = 15
KV = 5
HD = 64
FF = 2560
MB = 2
SEQ = 384
TOKENS = 6144


boundary_count = 2


def doc_layout(key):
    shape = (MB, TOKENS // SEQ, SEQ)
    token_index = jnp.arange(SEQ, dtype=jnp.int32)
    raw_scores = jax.random.randint(jax.random.fold_in(key, 11), shape, 0, 65536).astype(jnp.int32)
    scores = raw_scores * SEQ + token_index
    scores = jnp.where(token_index == 0, jnp.int32(2147483647), scores)
    ordered = jnp.sort(scores, axis=2)
    cutoff = ordered[:, :, boundary_count - 1:boundary_count]
    begins = (scores <= cutoff) | (token_index == 0)
    segment_ids = jnp.cumsum(begins.astype(jnp.int32), axis=2) - 1
    first_index = lax.cummax(jnp.where(begins, token_index, 0).astype(jnp.int32), axis=2)
    offsets = jax.random.randint(jax.random.fold_in(key, 12), shape, 0, 2048)
    start_offset = jnp.take_along_axis(offsets, first_index, axis=2)
    position_ids = token_index - first_index + start_offset
    return (segment_ids.reshape(MB, TOKENS).astype(jnp.int32), position_ids.reshape(MB, TOKENS).astype(jnp.int32))


def draw_segments(key, part):
    return doc_layout(key)[0]


def draw_positions(key, part):
    return doc_layout(key)[1]


def steps_of(stream_key, extent, split, low, high):
    def one(axis_at, shards_of):
        heights = jax.random.uniform(jax.random.fold_in(jax.random.fold_in(stream_key, 6), axis_at), (shards_of,), jnp.float32, low / len(split), high / len(split))
        return jnp.repeat(jnp.exp(heights), extent[axis_at] // shards_of).reshape((-1,) + (1,) * (len(extent) - axis_at - 1))

    level = one(*split[0])
    for cut in split[1:]:
        level = level * one(*cut)
    return level


def noise(own_key, dims, deviation, bound, pieces=(), kind=jnp.bfloat16):
    level = steps_of(own_key, dims, pieces, -0.22, 0.18) if pieces else 1.0
    drawn = jax.random.normal(own_key, dims, jnp.float32) * deviation * level
    return jnp.minimum(jnp.maximum(drawn, -bound), bound).astype(kind)


def setup_inputs(seed: int = 0) -> dict:
    key_list = jax.random.split(jax.random.key(seed), 14)
    inputs = noise(key_list[0], (MB, TOKENS, D), 1.0, 6.0, ((1, 16),))
    cotangent = noise(key_list[1], (MB, TOKENS, D), 1.0, 6.0, ((1, 16),), jnp.float32)
    segments = draw_segments(jax.random.fold_in(key_list[13], 71), 0)
    positions = draw_positions(jax.random.fold_in(key_list[13], 71), 0)
    norm_first = jnp.clip(1.0 + 0.18 * jax.random.normal(key_list[4], (2, D), jnp.float32), 0.099609375, 1.8984375).astype(jnp.bfloat16)
    w_query = noise(key_list[5], (2, D, HEADS * HD), D ** -0.5, 0.1875, ((0, 2), (1, 16)))
    w_key = noise(key_list[6], (2, D, KV * HD), D ** -0.5, 0.1875, ((0, 2), (1, 16)))
    w_value = noise(key_list[7], (2, D, KV * HD), D ** -0.5, 0.1875, ((0, 2), (1, 16)))
    w_out = noise(key_list[8], (2, HEADS * HD, D), (HEADS * HD // 8) ** -0.5, 0.5, ((0, 2), (1, 16)))
    norm_second = jnp.clip(1.0 + 0.18 * jax.random.normal(key_list[9], (2, D), jnp.float32), 0.099609375, 1.8984375).astype(jnp.bfloat16)
    w_gate = noise(key_list[10], (2, D, FF), D ** -0.5, 0.1875, ((0, 2), (1, 16)))
    w_up = noise(key_list[11], (2, D, FF), D ** -0.5, 0.1875, ((0, 2), (1, 16)))
    w_down = noise(key_list[12], (2, FF, D), FF ** -0.5, 0.125, ((0, 2), (1, 16)))
    return dict(inputs=inputs, cotangent=cotangent, segments=segments, positions=positions, norm_first=norm_first, w_query=w_query, w_key=w_key, w_value=w_value, w_out=w_out, norm_second=norm_second, w_gate=w_gate, w_up=w_up, w_down=w_down)


epsilon = 1e-05
rope_base = 100000.0

@jax.custom_vjp
def low(v):
    return lax.optimization_barrier(v.astype(jnp.bfloat16)).astype(jnp.float32)

@jax.custom_vjp
def low_back(v):
    return v

def low_keep(v):
    return (low(v), None)

def low_pass(kept, grad):
    return (grad,)

def back_keep(v):
    return (v, None)

def back_low(kept, grad):
    return (low(grad),)
low.defvjp(low_keep, low_pass)
low_back.defvjp(back_keep, back_low)

def exact_dot(left_side, right_side):
    return jnp.dot(left_side, right_side, precision=lax.Precision.HIGHEST, preferred_element_type=jnp.float32)

def rms_norm(values, gain_row):
    return values * lax.rsqrt(lax.optimization_barrier(jnp.mean(values * values, axis=-1, keepdims=True)) + epsilon) * gain_row

def rotate(values, places):
    half_dim = values.shape[-1] // 2
    frequency = rope_base ** (-jnp.arange(half_dim, dtype=jnp.float32) / half_dim)
    angles = places.astype(jnp.float32)[:, None, None] * frequency
    cosine = jnp.cos(angles)
    sine_part = jnp.sin(angles)
    front_half = values[..., :half_dim]
    back_half = values[..., half_dim:]
    return jnp.concatenate([front_half * cosine - back_half * sine_part, back_half * cosine + front_half * sine_part], axis=-1)

def attend(block_data):
    queries, key_rows, value_rows, labels = block_data
    length = labels.shape[0]
    scores = low_back(jnp.einsum('qkgd,pkd->kgqp', queries, key_rows, precision=lax.Precision.HIGHEST) * float(HD) ** (-0.5))
    token_order = jnp.arange(length)
    allowed = (labels[:, None] == labels[None, :]) & (token_order[:, None] >= token_order[None, :])
    scores = jnp.where(allowed, scores, -1e+30)
    shifted = jnp.exp(scores - lax.optimization_barrier(jnp.max(scores, axis=-1, keepdims=True)))
    probs_all = shifted / lax.optimization_barrier(jnp.sum(shifted, axis=-1, keepdims=True))
    return jnp.einsum('kgqp,pkd->qkgd', low(probs_all), value_rows, precision=lax.Precision.HIGHEST)

def layer(states, params, labels, places):
    gain_one, query_w, key_w, value_w, out_w, gain_two, gate_w, up_w, down_w = params
    rows_all = states.shape[0]
    group_size = HEADS // KV
    seq_count = rows_all // SEQ
    normed = low(rms_norm(states, gain_one))
    queries = low(rotate(low_back(exact_dot(normed, query_w)).reshape(rows_all, HEADS, HD), places))
    key_rows = low(rotate(low_back(exact_dot(normed, key_w)).reshape(rows_all, KV, HD), places))
    value_rows = low(low_back(exact_dot(normed, value_w)))
    mixed_heads = lax.map(jax.checkpoint(attend), (queries.reshape(seq_count, SEQ, KV, group_size, HD), key_rows.reshape(seq_count, SEQ, KV, HD), value_rows.reshape(seq_count, SEQ, KV, HD), labels))
    attended = low(low_back(mixed_heads.reshape(rows_all, HEADS * HD)))
    middle = states + low_back(exact_dot(attended, out_w))
    second = low(rms_norm(middle, gain_two))
    gate_val = low_back(exact_dot(second, gate_w))
    up_val = low_back(exact_dot(second, up_w))
    hidden = low(jax.nn.silu(gate_val) * up_val)
    return middle + low_back(exact_dot(hidden, down_w))

def reference(inputs, cotangent, segments, positions, norm_first, w_query, w_key, w_value, w_out, norm_second, w_gate, w_up, w_down):
    rows_all = MB * TOKENS
    labels = segments.reshape(rows_all // SEQ, SEQ)
    places = positions.reshape(rows_all)
    stacked = tuple((weight.astype(jnp.float32) for weight in (norm_first, w_query, w_key, w_value, w_out, norm_second, w_gate, w_up, w_down)))
    section_zero = tuple((weight[0] for weight in stacked))
    section_one = tuple((weight[1] for weight in stacked))
    start = inputs.astype(jnp.float32).reshape(rows_all, D)

    def run_layer(states, params):
        return layer(states, params, labels, places)
    first, pull_zero = jax.vjp(run_layer, start, section_zero)
    again, pull_one = jax.vjp(run_layer, first, section_one)
    grad_first, grads_one = pull_one(cotangent.reshape(rows_all, D))
    grad_start, grads_zero = pull_zero(grad_first)
    activations = jnp.stack([first, again]).reshape(2, MB, TOKENS, D)
    input_grads = jnp.stack([grad_start, grad_first]).reshape(2, MB, TOKENS, D)
    paired = [jnp.stack([zero_part, one_part]) for zero_part, one_part in zip(grads_zero, grads_one)]
    return (activations, input_grads, paired[0], paired[1], paired[2], paired[3], paired[4], paired[5], paired[6], paired[7], paired[8])
```

```python
import jax
import jax.numpy as jnp
from jax import lax
from jax.sharding import PartitionSpec as P

HEADS = 15
KV = 5
HD = 64
GROUP = HEADS // KV

bf16 = jnp.bfloat16
f32 = jnp.float32
epsilon = 1e-05
rope_base = 100000.0


def dot(a, b):
    return jnp.dot(a, b, preferred_element_type=f32)


def dot_tn(a, b):
    return lax.dot_general(a, b, (((0,), (0,)), ((), ())), preferred_element_type=f32)


def dot_nt(a, b):
    return lax.dot_general(a, b, (((1,), (1,)), ((), ())), preferred_element_type=f32)


def one_hot(rows, targets):
    count = targets.shape[0]
    row = lax.broadcasted_iota(jnp.int32, (rows, count), 0)
    return (row == targets[None, :]).astype(bf16)


def split_dot(a, pick):
    high = a.astype(bf16)
    low = (a - high.astype(f32)).astype(bf16)
    return dot(high, pick) + dot(low, pick)


def rope_tables(places):
    half = HD // 2
    frequency = rope_base ** (-jnp.arange(half, dtype=f32) / half)
    angles = places.astype(f32)[:, None] * frequency
    return jnp.cos(angles)[:, None, :], jnp.sin(angles)[:, None, :]


def rotate(values, cosine, sine):
    half = HD // 2
    front, back = values[..., :half], values[..., half:]
    return jnp.concatenate(
        [front * cosine - back * sine, back * cosine + front * sine], axis=-1
    )


def norm_scale(v, features):
    return lax.rsqrt(jnp.sum(v * v, axis=-1, keepdims=True) / features + epsilon)


def norm_back(v, scale, gain, grad, features):
    gain_grad = jnp.sum(grad * v * scale, axis=0)
    weighted = grad * gain
    mean = jnp.sum(weighted * v, axis=-1, keepdims=True) / features
    return scale * weighted - v * (scale * scale * scale) * mean, gain_grad


def forward(x, w, allowed, tables, spread, features):
    length = x.shape[0]
    scale_one = norm_scale(x, features)
    normed = (x * scale_one * w["gain_one"]).astype(bf16)
    qkv = dot(normed, w["qkv"])
    wide = HEADS * HD
    narrow = KV * HD
    queries = rotate(qkv[:, :wide].reshape(length, HEADS, HD), *tables).astype(bf16)
    queries = queries.reshape(length, KV, GROUP, HD)
    keys = rotate(qkv[:, wide : wide + narrow].reshape(length, KV, HD), *tables).astype(bf16)
    values = qkv[:, wide + narrow : wide + 2 * narrow].astype(bf16).reshape(length, KV, HD)
    scores = jnp.einsum("qkgd,pkd->kgqp", queries, keys, preferred_element_type=f32)
    scores = jnp.where(allowed, scores * float(HD) ** (-0.5), -1e30)
    shifted = jnp.exp(scores - jnp.max(scores, axis=-1, keepdims=True))
    probs = shifted / jnp.sum(shifted, axis=-1, keepdims=True)
    attended = jnp.einsum(
        "kgqp,pkd->qkgd", probs.astype(bf16), values, preferred_element_type=f32
    )
    attended = dot(attended.reshape(length, wide).astype(bf16), spread).astype(bf16)
    middle = x + dot(attended, w["out"])
    scale_two = norm_scale(middle, features)
    second = (middle * scale_two * w["gain_two"]).astype(bf16)
    gate = dot(second, w["gate"])
    up = dot(second, w["up"])
    hidden = (jax.nn.silu(gate) * up).astype(bf16)
    output = middle + dot(hidden, w["down"])
    return output, (
        scale_one, normed, queries, keys, values, probs, attended, middle, scale_two, second, gate, up, hidden,
    )


def backward(x, w, tables, spread, features, kept, grad, emit):
    (scale_one, normed, queries, keys, values, probs, attended, middle, scale_two, second, gate, up, hidden) = kept
    length = x.shape[0]
    wide = HEADS * HD
    root = float(HD) ** (-0.5)
    low = grad.astype(bf16)
    emit("down", hidden, low)
    grad_hidden = dot_nt(low, w["down"])
    sig = jax.nn.sigmoid(gate)
    silu = gate * sig
    gate_low = (grad_hidden * up * (sig * (1.0 + gate * (1.0 - sig)))).astype(bf16)
    up_low = (grad_hidden * silu).astype(bf16)
    emit("gate_up", second, jnp.concatenate([gate_low, up_low], axis=1))
    grad_second = dot_nt(gate_low, w["gate"]) + dot_nt(up_low, w["up"])
    grad_norm, gain_two = norm_back(middle, scale_two, w["gain_two"], grad_second, features)
    grad_middle = grad + grad_norm
    middle_low = grad_middle.astype(bf16)
    grad_att = dot_nt(middle_low, w["out"]).astype(bf16)
    grad_att = dot_nt(grad_att, spread).astype(bf16).reshape(length, KV, GROUP, HD)
    grad_probs = jnp.einsum("qkgd,pkd->kgqp", grad_att, values, preferred_element_type=f32)
    grad_values = (
        jnp.einsum("kgqp,qkgd->pkd", probs.astype(bf16), grad_att, preferred_element_type=f32)
        .reshape(length, KV * HD)
        .astype(bf16)
    )
    scores_low = (
        probs * (grad_probs - jnp.sum(probs * grad_probs, axis=-1, keepdims=True))
    ).astype(bf16)
    turned_q = jnp.einsum("kgqp,pkd->qkgd", scores_low, keys, preferred_element_type=f32) * root
    turned_k = jnp.einsum("kgqp,qkgd->pkd", scores_low, queries, preferred_element_type=f32) * root
    cosine, sine = tables
    grad_q = rotate(turned_q.reshape(length, HEADS, HD), cosine, -sine).astype(bf16)
    grad_k = rotate(turned_k, cosine, -sine).astype(bf16)
    grad_qkv = jnp.concatenate(
        [grad_q.reshape(length, wide), grad_k.reshape(length, KV * HD), grad_values], axis=1
    )
    grad_normed = dot_nt(grad_qkv, w["qkv"])
    grad_norm, gain_one = norm_back(x, scale_one, w["gain_one"], grad_normed, features)
    emit("attention", (normed, attended), (grad_qkv, middle_low, gain_one, gain_two))
    return grad_middle + grad_norm


class Halves:
    def __init__(self, n, features, hidden):
        self.n, self.features, self.hidden = n, features, hidden
        self.parts = 2 * n
        self.rows = features // self.parts
        self.padded = -(-self.rows // 16) * 16
        self.wide = self.parts * self.padded
        self.down_rows = hidden // self.parts
        self.section = lax.axis_index("section")
        self.first = self.section == 0
        self.place = lax.axis_index("fsdp")
        lane = jnp.arange(self.wide, dtype=jnp.int32)
        inside = lane % self.padded
        natural = jnp.where(inside < self.rows, lane // self.padded * self.rows + inside, -1)
        self.spread = one_hot(features, natural)
        self.y = self.place // 2 % 2
        self.x = self.place % 2
        self.relative = self.relative_order()

    def permuted_hidden(self, array):
        rows = array.shape[0]
        blocks = array.reshape(rows, self.parts, self.down_rows)
        cut = self.padded
        return jnp.concatenate(
            [
                blocks[:, :, :cut].reshape(rows, -1),
                blocks[:, :, cut : 2 * cut].reshape(rows, -1),
                blocks[:, :, 2 * cut :].reshape(rows, -1),
            ],
            axis=1,
        )

    def natural_hidden(self, array):
        rows = array.shape[0]
        cut = self.padded
        third = self.down_rows - 2 * cut
        one = array[:, : self.wide].reshape(rows, self.parts, cut)
        two = array[:, self.wide : 2 * self.wide].reshape(rows, self.parts, cut)
        three = array[:, 2 * self.wide :].reshape(rows, self.parts, third)
        return jnp.concatenate([one, two, three], axis=2).reshape(rows, self.hidden)

    def swap(self, array):
        return lax.ppermute(array, "section", [(0, 1), (1, 0)])

    def packed(self, weights):
        gain_one, query, key, value, out, gain_two, gate, up, down = weights
        self.wide_qkv = query.shape[1] + key.shape[1] + value.shape[1]
        self.cols_qkv = -(-(self.wide_qkv + 2) // 128) * 128
        spare = self.cols_qkv - self.wide_qkv - 2
        rows = query.shape[0]
        half = self.wide // 2
        columns = jnp.concatenate(
            [
                query, key, value, gain_one[:, None], gain_two[:, None], jnp.zeros((rows, spare), bf16),
                dot(out, self.spread).astype(bf16),
                self.permuted_hidden(gate), self.permuted_hidden(up),
            ],
            axis=1,
        ).reshape(2, self.rows, -1)
        columns = jnp.pad(columns, ((0, 0), (0, self.padded - self.rows), (0, 0)))
        down = dot(down, self.spread).astype(bf16).reshape(2, self.down_rows, self.wide)
        cut = self.padded
        last = down[:, 2 * cut :]
        last = jnp.concatenate([last[:, :, :half], last[:, :, half:]], axis=1)
        return jnp.concatenate([columns, down[:, :cut], down[:, cut : 2 * cut], last], axis=2)

    def gathered(self, weights):
        halves = self.packed(weights)
        keep = jnp.where(self.first, halves[0], halves[1])
        got = self.swap(jnp.where(self.first, halves[1], halves[0]))
        carried = (jnp.where(self.first, keep, got), jnp.where(self.first, got, keep))
        return [
            self.unpacked(lax.all_gather(part, ("fsdp", "section"), axis=0, tiled=True))
            for part in carried
        ]

    def unpacked(self, whole):
        a = self.cols_qkv
        b = a + self.wide
        c = b + self.hidden
        d = c + self.hidden
        half = self.wide // 2
        gains = whole[:, self.wide_qkv : self.wide_qkv + 2].astype(f32).T
        cut = self.padded
        last = whole[:, d + 2 * self.wide :].reshape(self.parts, 2, cut // 2, half)
        last = last.transpose(0, 2, 1, 3).reshape(self.parts * (cut // 2), self.wide)
        return {
            "qkv": whole[:, : self.wide_qkv],
            "gain_one": gains[0],
            "gain_two": gains[1],
            "out": whole[:, a:b],
            "gate": whole[:, b:c],
            "up": whole[:, c:d],
            "down": jnp.concatenate(
                [whole[:, d : d + self.wide], whole[:, d + self.wide : d + 2 * self.wide], last], axis=0
            ),
        }

    def relative_order(self):
        block = jnp.arange(self.parts, dtype=jnp.int32)
        z = block % (self.n // 4)
        quarter = block // (self.n // 4) % 4
        core = self.section ^ (block // self.n)
        low, high = quarter % 2, quarter // 2
        other_x = jnp.where(core == 0, low, high)
        other_y = jnp.where(core == 0, high, low)
        chip = z * 4 + (self.y ^ other_y) * 2 + (self.x ^ other_x)
        return chip * 2 + core

    def order_matrices(self):
        lane = jnp.arange(self.wide, dtype=jnp.int32)
        part = jnp.repeat(self.relative, self.padded)
        inside = lane % self.padded
        half = self.padded // 2
        return (
            one_hot(self.wide, part * self.padded + inside),
            one_hot(self.wide // 2, jnp.where(inside < half, part * half + inside, -1)),
            one_hot(self.wide // 2, jnp.where(inside >= half, part * half + inside - half, -1)),
        )

    def routes(self):
        flips = {"x": 1, "y": 2}
        count = self.n

        def route(by_core):
            return [
                (core * count + i, core * count + (i ^ flips[axis]))
                for core, axis in enumerate(by_core)
                for i in range(count)
            ]

        return route("yx"), route("xy")

    def reduced(self, terms, columns=None):
        half = self.wide // 2

        def product(lo, hi):
            return jnp.concatenate(
                [dot_tn(a[:, lo:hi], b) for a, b in terms]
                + ([columns[lo:hi]] if columns is not None else []),
                axis=1,
            )

        first_route, second_route = self.routes()
        got = self.swap(product(half, self.wide).astype(bf16))
        mine = (product(0, half) + got.astype(f32)).astype(bf16)
        got = lax.ppermute(mine[half // 2 :], ("section", "fsdp"), first_route)
        mine = (mine[: half // 2].astype(f32) + got.astype(f32)).astype(bf16)
        got = lax.ppermute(mine[half // 4 :], ("section", "fsdp"), second_route)
        mine = (mine[: half // 4].astype(f32) + got.astype(f32)).astype(bf16)
        lines = [[q + 4 * z for z in range(self.n // 4)] for q in range(4)]
        return lax.psum_scatter(mine, "fsdp", scatter_dimension=0, tiled=True, axis_index_groups=lines)

    def emitter(self):
        whole, left, right = self.order_matrices()
        sums = {}
        half = self.wide // 2

        def order(a, pick):
            return dot(a, pick).astype(bf16)

        def emit(name, lhs, rhs):
            if name == "down":
                last = lhs[:, 2 * self.wide :]
                both = jnp.concatenate([order(last, left), order(last, right)], axis=0)
                sides = jnp.concatenate([rhs[:, :half], rhs[:, half:]], axis=0)
                terms = [
                    (order(lhs[:, : self.wide], whole), rhs),
                    (order(lhs[:, self.wide : 2 * self.wide], whole), rhs),
                    (both, sides),
                ]
                sums[name] = self.reduced(terms)
            elif name == "gate_up":
                sums[name] = self.reduced([(order(lhs, whole), rhs)])
            else:
                normed, attended = lhs
                grad_qkv, middle_low, gain_one, gain_two = rhs
                gains = dot_tn(whole, jnp.stack([gain_one, gain_two], axis=1).astype(bf16))
                spare = jnp.zeros((self.wide, self.cols_qkv - self.wide_qkv - 2), f32)
                sums[name] = self.reduced(
                    [(order(attended, whole), middle_low), (order(normed, whole), grad_qkv)],
                    jnp.concatenate([gains, spare], axis=1),
                )

        return emit, sums

    def shares(self, sums):
        result = []
        for name in ("down", "gate_up", "attention"):
            zero, one = sums[0][name], sums[1][name]
            keep = jnp.where(self.first, zero, one)
            got = self.swap(jnp.where(self.first, one, zero))
            result.append(
                jnp.stack([jnp.where(self.first, keep, got), jnp.where(self.first, got, keep)]).astype(f32)
            )
        down, gate_up, attention = result
        half = self.wide // 2
        cut = self.padded
        last = down[:, :, 2 * self.wide :]
        last = jnp.concatenate([last[:, : cut // 2], last[:, cut // 2 :]], axis=2)
        down = jnp.concatenate([down[:, :, : self.wide], down[:, :, self.wide : 2 * self.wide], last], axis=1)
        down = self.natural_features(down.reshape(2 * self.down_rows, self.wide))
        gate_up = gate_up[:, : self.rows].reshape(2 * self.rows, -1)
        attention = attention[:, : self.rows].reshape(2 * self.rows, -1)
        out = self.natural_features(attention[:, : self.wide])
        qkv = attention[:, self.wide :]
        wide, narrow = HEADS * HD, KV * HD
        return (
            qkv[:, self.wide_qkv],
            qkv[:, :wide],
            qkv[:, wide : wide + narrow],
            qkv[:, wide + narrow : wide + 2 * narrow],
            out,
            qkv[:, self.wide_qkv + 1],
            self.natural_hidden(gate_up[:, : self.hidden]),
            self.natural_hidden(gate_up[:, self.hidden :]),
            down,
        )

    def natural_features(self, array):
        return dot_nt(array.astype(bf16), self.spread)


class Plain:
    def __init__(self, n, features, hidden):
        self.features, self.wide = features, features
        self.first = lax.axis_index("section") == 0
        self.spread = one_hot(features, jnp.arange(features, dtype=jnp.int32))

    def gathered(self, weights):
        names = ("gain_one", "query", "key", "value", "out", "gain_two", "gate", "up", "down")
        both = [lax.all_gather(part, ("section", "fsdp"), axis=0, tiled=True) for part in weights]
        layers = []
        for layer in range(2):
            w = {name: a.reshape((2, -1) + a.shape[1:])[layer] for name, a in zip(names, both)}
            w["qkv"] = jnp.concatenate([w["query"], w["key"], w["value"]], axis=1)
            w["gain_one"] = w["gain_one"].astype(f32)
            w["gain_two"] = w["gain_two"].astype(f32)
            layers.append(w)
        return layers

    def emitter(self):
        sums = {}

        def reduced(a):
            part = lax.psum_scatter(a, "fsdp", scatter_dimension=0, tiled=True)
            return lax.psum(part, "section")

        def emit(name, lhs, rhs):
            if name == "attention":
                normed, attended = lhs
                grad_qkv, middle_low, gain_one, gain_two = rhs
                sums["out"] = reduced(dot_tn(attended, middle_low))
                sums["qkv"] = reduced(dot_tn(normed, grad_qkv))
                sums["gain_one"] = reduced(gain_one)
                sums["gain_two"] = reduced(gain_two)
            else:
                sums[name] = reduced(dot_tn(lhs, rhs))

        return emit, sums

    def shares(self, sums):
        own = {name: jnp.where(self.first, sums[0][name], sums[1][name]) for name in sums[0]}
        wide, narrow = HEADS * HD, KV * HD
        hidden = own["gate_up"].shape[1] // 2
        return (
            own["gain_one"],
            own["qkv"][:, :wide],
            own["qkv"][:, wide : wide + narrow],
            own["qkv"][:, wide + narrow :],
            own["out"],
            own["gain_two"],
            own["gate_up"][:, :hidden],
            own["gate_up"][:, hidden:],
            own["down"],
        )


def on_device(inputs, cotangent, segments, positions, *weights):
    n = lax.axis_size("fsdp")
    features = inputs.shape[-1]
    hidden = weights[6].shape[-1]
    fits = n == 16 and features == 960 and hidden == 2560
    plan = (Halves if fits else Plain)(n, features, hidden)
    section = lax.axis_index("section")
    first = section == 0
    layers = plan.gathered([weight[0] for weight in weights])
    spread = plan.spread

    def mine(array):
        return lax.dynamic_index_in_dim(array, section, 0, keepdims=False)

    labels = mine(segments)
    length = labels.shape[0]
    token = jnp.arange(length)
    allowed = (labels[:, None] == labels[None, :]) & (token[:, None] >= token[None, :])
    tables = rope_tables(mine(positions))

    start = dot(mine(inputs), spread)
    middle, kept_zero = forward(start, layers[0], allowed, tables, spread, features)
    end, kept_one = forward(middle, layers[1], allowed, tables, spread, features)

    grad = split_dot(mine(cotangent), spread)
    emit_one, sums_one = plan.emitter()
    grad_middle = backward(middle, layers[1], tables, spread, features, kept_one, grad, emit_one)
    emit_zero, sums_zero = plan.emitter()
    grad_start = backward(start, layers[0], tables, spread, features, kept_zero, grad_middle, emit_zero)

    def exchanged(zero, one):
        keep = jnp.where(first, zero, one)
        sent = jnp.where(first, one, zero).astype(bf16)
        got = lax.ppermute(sent, "section", [(0, 1), (1, 0)])
        kept = keep.astype(bf16)
        rest = (keep - kept.astype(f32)).astype(bf16)
        kept = dot_nt(kept, spread) + dot_nt(rest, spread)
        got = dot_nt(got, spread)
        return jnp.stack([jnp.where(first, kept, got), jnp.where(first, got, kept)])[None]

    activations = exchanged(middle, end)
    input_grads = exchanged(grad_start, grad_middle)
    shares = plan.shares((sums_zero, sums_one))
    return (activations, input_grads) + tuple(share[None] for share in shares)


def solution(mesh):
    rows = P("section", "fsdp")
    matrix = P("section", "fsdp", None)
    weights = (rows, matrix, matrix, matrix, matrix, rows, matrix, matrix, matrix)
    tokens = P(None, "fsdp", None)
    return jax.shard_map(
        on_device,
        mesh=mesh,
        in_specs=(tokens, tokens, P(None, "fsdp"), P(None, "fsdp")) + weights,
        out_specs=(P("section", None, "fsdp", None), P("section", None, "fsdp", None)) + weights,
        check_vma=False,
    )
```

```python
import jax
import jax.numpy as jnp
from jax import lax
from jax.sharding import PartitionSpec as P

HEADS = 15
KV = 5
HD = 64
GROUP = HEADS // KV

bf16 = jnp.bfloat16
f32 = jnp.float32
epsilon = 1e-05
rope_base = 100000.0


def dot(a, b):
    return jnp.dot(a, b, preferred_element_type=f32)


def dot_tn(a, b):
    return lax.dot_general(a, b, (((0,), (0,)), ((), ())), preferred_element_type=f32)


def dot_nt(a, b):
    return lax.dot_general(a, b, (((1,), (1,)), ((), ())), preferred_element_type=f32)


def one_hot(rows, targets):
    count = targets.shape[0]
    row = lax.broadcasted_iota(jnp.int32, (rows, count), 0)
    return (row == targets[None, :]).astype(bf16)


def split_dot(a, pick):
    high = a.astype(bf16)
    low = (a - high.astype(f32)).astype(bf16)
    return dot(high, pick) + dot(low, pick)


def rope_tables(places):
    half = HD // 2
    frequency = rope_base ** (-jnp.arange(half, dtype=f32) / half)
    angles = places.astype(f32)[:, None] * frequency
    return jnp.cos(angles)[:, None, :], jnp.sin(angles)[:, None, :]


def rotate(values, cosine, sine):
    half = HD // 2
    front, back = values[..., :half], values[..., half:]
    return jnp.concatenate(
        [front * cosine - back * sine, back * cosine + front * sine], axis=-1
    )


def norm_scale(v, features):
    return lax.rsqrt(jnp.sum(v * v, axis=-1, keepdims=True) / features + epsilon)


def norm_back(v, scale, gain, grad, features):
    gain_grad = jnp.sum(grad * v * scale, axis=0)
    weighted = grad * gain
    mean = jnp.sum(weighted * v, axis=-1, keepdims=True) / features
    return scale * weighted - v * (scale * scale * scale) * mean, gain_grad


def forward(x, source, allowed, tables, features):
    length = x.shape[0]
    wide = HEADS * HD
    narrow = KV * HD
    for name in ("attention", "gate_up", "attention", "down", "attention", "gate_up", "attention"):
        x = source.tie(x, name)
    w = source.weights("attention")
    scale_one = norm_scale(x, features)
    normed = w["order"]((x * scale_one * w["gain_one"]).astype(bf16))
    qkv = dot(normed, w["qkv"])
    qkv = source.tie(qkv, "down")
    queries = rotate(qkv[:, :wide].reshape(length, HEADS, HD), *tables).astype(bf16)
    queries = queries.reshape(length, KV, GROUP, HD)
    keys = rotate(qkv[:, wide : wide + narrow].reshape(length, KV, HD), *tables).astype(bf16)
    values = qkv[:, wide + narrow : wide + 2 * narrow].astype(bf16).reshape(length, KV, HD)
    scores = jnp.einsum("qkgd,pkd->kgqp", queries, keys, preferred_element_type=f32)
    scores = jnp.where(allowed, scores * float(HD) ** (-0.5), -1e30)
    shifted = jnp.exp(scores - jnp.max(scores, axis=-1, keepdims=True))
    probs = shifted / jnp.sum(shifted, axis=-1, keepdims=True)
    attended = jnp.einsum(
        "kgqp,pkd->qkgd", probs.astype(bf16), values, preferred_element_type=f32
    )
    attended = dot(attended.reshape(length, wide).astype(bf16), w["spread"]).astype(bf16)
    attended = source.tie(attended, "gate_up")
    middle = x + dot(attended, w["out"])
    middle = source.tie(middle, "gate_up")
    w.update(source.weights("gate_up"))
    scale_two = norm_scale(middle, features)
    second = w["order"]((middle * scale_two * w["gain_two"]).astype(bf16))
    gate = dot(second, w["gate"])
    up = dot(second, w["up"])
    hidden = (jax.nn.silu(gate) * up).astype(bf16)
    hidden = source.tie(hidden, "down")
    hidden = source.tie(hidden, "down")
    w.update(source.weights("down"))
    hidden = w["order_hidden"](hidden)
    output = middle + dot(hidden, w["down"])
    return output, w, (
        scale_one, normed, queries, keys, values, probs, attended, middle, scale_two, second, gate, up, hidden,
    )


def backward(x, w, tables, features, kept, grad, flow):
    (scale_one, normed, queries, keys, values, probs, attended, middle, scale_two, second, gate, up, hidden) = kept
    length = x.shape[0]
    wide = HEADS * HD
    root = float(HD) ** (-0.5)
    low = grad.astype(bf16)
    flow.begin("down", w["relative_hidden"](hidden), low)
    grad_hidden = w["back_hidden"](dot_nt(low, w["down"]))
    sig = jax.nn.sigmoid(gate)
    silu = gate * sig
    gate_low = (grad_hidden * up * (sig * (1.0 + gate * (1.0 - sig)))).astype(bf16)
    up_low = (grad_hidden * silu).astype(bf16)
    gate_low, up_low = flow.tie((gate_low, up_low), "down", "+attention", "+gate_up")
    flow.begin("gate_up", w["relative"](second), jnp.concatenate([gate_low, up_low], axis=1))
    grad_second = dot_nt(gate_low, w["gate"]) + dot_nt(up_low, w["up"])
    grad_second = w["back"](grad_second)
    grad_norm, gain_two = norm_back(middle, scale_two, w["gain_two"], grad_second, features)
    grad_middle = grad + grad_norm
    grad_middle = flow.tie(grad_middle, "gate_up", "down", "+attention")
    middle_low = grad_middle.astype(bf16)
    grad_att = dot_nt(middle_low, w["out"]).astype(bf16)
    grad_att = dot_nt(grad_att, w["spread"]).astype(bf16).reshape(length, KV, GROUP, HD)
    grad_probs = jnp.einsum("qkgd,pkd->kgqp", grad_att, values, preferred_element_type=f32)
    grad_values = (
        jnp.einsum("kgqp,qkgd->pkd", probs.astype(bf16), grad_att, preferred_element_type=f32)
        .reshape(length, KV * HD)
        .astype(bf16)
    )
    scores_low = (
        probs * (grad_probs - jnp.sum(probs * grad_probs, axis=-1, keepdims=True))
    ).astype(bf16)
    scores_low = flow.tie(scores_low, "down")
    turned_q = jnp.einsum("kgqp,pkd->qkgd", scores_low, keys, preferred_element_type=f32) * root
    turned_k = jnp.einsum("kgqp,qkgd->pkd", scores_low, queries, preferred_element_type=f32) * root
    cosine, sine = tables
    grad_q = rotate(turned_q.reshape(length, HEADS, HD), cosine, -sine).astype(bf16)
    grad_k = rotate(turned_k, cosine, -sine).astype(bf16)
    grad_qkv = jnp.concatenate(
        [grad_q.reshape(length, wide), grad_k.reshape(length, KV * HD), grad_values], axis=1
    )
    grad_qkv = flow.tie(grad_qkv, "gate_up")
    grad_normed = w["back"](dot_nt(grad_qkv, w["qkv"]))
    grad_norm, gain_one = norm_back(x, scale_one, w["gain_one"], grad_normed, features)
    flow.begin("attention", (w["relative"](normed), w["relative"](attended)), (grad_qkv, middle_low, gain_one, gain_two))
    grad = flow.tie(grad_middle + grad_norm, "attention")
    flow.next_layer()
    return grad


class Arriving:
    def __init__(self, steps, unpack):
        self.table = {name: (one, next(one)) for name, one in steps.items()}
        self.unpack = unpack

    def tie(self, value, name):
        steps, waited = self.table[name]
        if steps is None:
            return value
        value, got = lax.optimization_barrier((value, waited))
        try:
            self.table[name] = (steps, steps.send(got))
        except StopIteration as end:
            self.table[name] = (None, end.value)
        return value

    def weights(self, name):
        while self.table[name][0] is not None:
            self.tie((), name)
        return self.unpack(name, self.table[name][1])


class Flow:
    def __init__(self, begin):
        self.begun = begin
        self.now, self.before, self.done = {}, {}, []

    def begin(self, name, lhs, rhs):
        steps = self.begun(name, lhs, rhs)
        self.now[name] = (steps, next(steps))

    def tie(self, value, *names):
        tables = [(self.before, n[1:]) if n.startswith("+") else (self.now, n) for n in names]
        tables = [(table, n) for table, n in tables if n in table and table[n][0] is not None]
        value, waited = lax.optimization_barrier((value, [table[n][1] for table, n in tables]))
        for (table, n), got in zip(tables, waited):
            self.advance(table, n, got)
        return value

    def advance(self, table, name, got):
        steps = table[name][0]
        try:
            table[name] = (steps, steps.send(got))
        except StopIteration as end:
            table[name] = (None, end.value)

    def next_layer(self):
        self.done.append(self.before)
        self.before, self.now = self.now, {}

    def finished(self):
        self.next_layer()
        tables = self.done[1:]
        for table in tables:
            while any(steps is not None for steps, _ in table.values()):
                for name in table:
                    if table[name][0] is not None:
                        self.advance(table, name, table[name][1])
        return [{name: value for name, (_, value) in table.items()} for table in tables]


class Halves:
    def __init__(self, n, features, hidden):
        self.n, self.features, self.hidden = n, features, hidden
        self.parts = 2 * n
        self.rows = features // self.parts
        self.padded = -(-self.rows // 16) * 16
        self.wide = self.parts * self.padded
        self.down_rows = hidden // self.parts
        self.section = lax.axis_index("section")
        self.first = self.section == 0
        self.place = lax.axis_index("fsdp")
        lane = jnp.arange(self.wide, dtype=jnp.int32)
        inside = lane % self.padded
        natural = jnp.where(inside < self.rows, lane // self.padded * self.rows + inside, -1)
        self.spread = one_hot(features, natural)
        self.y = self.place // 2 % 2
        self.x = self.place % 2
        self.relative = self.relative_order()

    def permuted_hidden(self, array):
        rows = array.shape[0]
        blocks = array.reshape(rows, self.parts, self.down_rows)
        cut = self.padded
        return jnp.concatenate(
            [
                blocks[:, :, :cut].reshape(rows, -1),
                blocks[:, :, cut : 2 * cut].reshape(rows, -1),
                blocks[:, :, 2 * cut :].reshape(rows, -1),
            ],
            axis=1,
        )

    def natural_hidden(self, array):
        rows = array.shape[0]
        cut = self.padded
        third = self.down_rows - 2 * cut
        one = array[:, : self.wide].reshape(rows, self.parts, cut)
        two = array[:, self.wide : 2 * self.wide].reshape(rows, self.parts, cut)
        three = array[:, 2 * self.wide :].reshape(rows, self.parts, third)
        return jnp.concatenate([one, two, three], axis=2).reshape(rows, self.hidden)

    def swap(self, array):
        return lax.ppermute(array, "section", [(0, 1), (1, 0)])

    def packed(self, weights):
        gain_one, query, key, value, out, gain_two, gate, up, down = weights
        self.wide_qkv = query.shape[1] + key.shape[1] + value.shape[1]
        self.cols_qkv = -(-(self.wide_qkv + 2) // 128) * 128
        spare = self.cols_qkv - self.wide_qkv - 2
        rows = query.shape[0]
        half = self.wide // 2

        def halves(parts):
            both = jnp.concatenate(parts, axis=1).reshape(2, self.rows, -1)
            return jnp.pad(both, ((0, 0), (0, self.padded - self.rows), (0, 0)))

        down = dot(down, self.spread).astype(bf16).reshape(2, self.down_rows, self.wide)
        cut = self.padded
        last = down[:, 2 * cut :]
        last = jnp.concatenate([last[:, :, :half], last[:, :, half:]], axis=1)
        return {
            "attention": halves([
                query, key, value, gain_one[:, None], gain_two[:, None], jnp.zeros((rows, spare), bf16),
                dot(out, self.spread).astype(bf16),
            ]),
            "gate_up": halves([self.permuted_hidden(gate), self.permuted_hidden(up)]),
            "down": jnp.concatenate([down[:, :cut], down[:, cut : 2 * cut], last], axis=2),
        }

    def sources(self, weights):
        carried = {}
        for name, halves in self.packed(weights).items():
            keep = jnp.where(self.first, halves[0], halves[1])
            got = self.swap(jnp.where(self.first, halves[1], halves[0]))
            carried[name] = (jnp.where(self.first, keep, got), jnp.where(self.first, got, keep))
        names = ("attention", "gate_up", "down")
        whole, left, right = self.order_matrices()
        both = self.wide

        def to_relative(a):
            return dot(a, whole).astype(bf16)

        def hidden_to_relative(a):
            last = a[:, 2 * both :]
            return jnp.concatenate(
                [
                    to_relative(a[:, :both]),
                    to_relative(a[:, both : 2 * both]),
                    dot(last, self.order_last).astype(bf16),
                ],
                axis=1,
            )

        def from_relative(a):
            high = a.astype(bf16)
            low = (a - high.astype(f32)).astype(bf16)
            return dot_nt(high, whole) + dot_nt(low, whole)

        def hidden_from_relative(a):
            a = a.astype(bf16)
            return jnp.concatenate(
                [
                    dot_nt(a[:, :both], whole),
                    dot_nt(a[:, both : 2 * both], whole),
                    dot_nt(a[:, 2 * both :], self.order_last),
                ],
                axis=1,
            )

        def same(a):
            return a

        moved = {
            "order": to_relative, "order_hidden": hidden_to_relative, "relative": same,
            "relative_hidden": same, "back": from_relative, "back_hidden": hidden_from_relative,
            "spread": dot(self.spread, whole).astype(bf16),
        }
        straight = {
            "order": same, "order_hidden": same, "relative": to_relative,
            "relative_hidden": hidden_to_relative, "back": same, "back_hidden": same,
            "spread": self.spread,
        }

        def unpack_moved(name, a):
            w = self.unpacked(name, a)
            if name == "attention":
                gains = dot(whole, a[:, self.wide_qkv : self.cols_qkv])[:, :2].T
                w.update(moved, gain_one=gains[0], gain_two=gains[1])
            return w

        def unpack_straight(name, a):
            w = self.unpacked(name, a)
            if name == "attention":
                gains = a[:, self.wide_qkv : self.wide_qkv + 2].astype(f32).T
                w.update(straight, gain_one=gains[0], gain_two=gains[1])
            return w

        def one_gather():
            sent = jnp.concatenate([carried[name][1] for name in names], axis=1)
            return lax.all_gather(sent, ("fsdp", "section"), axis=0, tiled=True)

        gathered = one_gather()
        widths = [carried[name][1].shape[1] for name in names]

        def column(index):
            at = sum(widths[:index])
            yield ()
            return gathered[:, at : at + widths[index]]

        return (
            Arriving({name: self.travelled(carried[name][0]) for name in names}, unpack_moved),
            Arriving({name: column(index) for index, name in enumerate(names)}, unpack_straight),
        )

    def travelled(self, part):
        depth = self.n // 4
        got = yield [
            lax.ppermute(part, "fsdp", [(i, (i + 4 * k) % self.n) for i in range(self.n)])
            for k in range(1, depth)
        ]
        ring = [part] + list(got)
        turned = jnp.concatenate([ring[(depth - 1 - k) % depth] for k in range(2 * depth - 1)], axis=0)
        z = self.place // 4
        line = lax.dynamic_slice_in_dim(turned, (depth - 1 - z) * self.padded, depth * self.padded, 0)
        first_route, second_route = self.routes()
        got = yield lax.ppermute(line, ("section", "fsdp"), second_route)
        pair = jnp.concatenate([line, got], axis=0)
        got = yield lax.ppermute(pair, ("section", "fsdp"), first_route)
        mine = jnp.concatenate([pair, got], axis=0)
        got = yield self.swap(mine)
        return jnp.concatenate([mine, got], axis=0)

    def unpacked(self, name, whole):
        if name == "attention":
            return {"qkv": whole[:, : self.wide_qkv], "out": whole[:, self.cols_qkv :]}
        if name == "gate_up":
            return {"gate": whole[:, : self.hidden], "up": whole[:, self.hidden :]}
        half = self.wide // 2
        cut = self.padded
        last = whole[:, 2 * self.wide :].reshape(self.parts, 2, cut // 2, half)
        last = last.transpose(0, 2, 1, 3).reshape(self.parts * (cut // 2), self.wide)
        return {
            "down": jnp.concatenate([whole[:, : self.wide], whole[:, self.wide : 2 * self.wide], last], axis=0)
        }

    def relative_order(self):
        block = jnp.arange(self.parts, dtype=jnp.int32)
        z = block % (self.n // 4)
        quarter = block // (self.n // 4) % 4
        core = self.section ^ (block // self.n)
        low, high = quarter % 2, quarter // 2
        other_x = jnp.where(core == 0, low, high)
        other_y = jnp.where(core == 0, high, low)
        chip = z * 4 + (self.y ^ other_y) * 2 + (self.x ^ other_x)
        return chip * 2 + core

    def order_matrices(self):
        lane = jnp.arange(self.wide, dtype=jnp.int32)
        part = jnp.repeat(self.relative, self.padded)
        inside = lane % self.padded
        half = self.padded // 2
        block = lane // self.padded * half
        short = jnp.arange(self.wide // 2, dtype=jnp.int32)
        self.order_last = one_hot(self.wide // 2, jnp.repeat(self.relative, half) * half + short % half)
        return (
            one_hot(self.wide, part * self.padded + inside),
            one_hot(self.wide // 2, jnp.where(inside < half, block + inside, -1)),
            one_hot(self.wide // 2, jnp.where(inside >= half, block + inside - half, -1)),
        )

    def routes(self):
        flips = {"x": 1, "y": 2}
        count = self.n

        def route(by_core):
            return [
                (core * count + i, core * count + (i ^ flips[axis]))
                for core, axis in enumerate(by_core)
                for i in range(count)
            ]

        return route("yx"), route("xy")

    def reduced(self, terms, columns=None):
        half = self.wide // 2

        def product(lo, hi):
            return jnp.concatenate(
                [dot_tn(a[:, lo:hi], b) for a, b in terms]
                + ([columns[lo:hi]] if columns is not None else []),
                axis=1,
            )

        first_route, second_route = self.routes()
        got = yield self.swap(product(half, self.wide).astype(bf16))
        mine = (product(0, half) + got.astype(f32)).astype(bf16)
        got = yield lax.ppermute(mine[half // 2 :], ("section", "fsdp"), first_route)
        mine = (mine[: half // 2].astype(f32) + got.astype(f32)).astype(bf16)
        got = yield lax.ppermute(mine[half // 4 :], ("section", "fsdp"), second_route)
        mine = (mine[: half // 4].astype(f32) + got.astype(f32)).astype(bf16)
        lines = [[q + 4 * z for z in range(self.n // 4)] for q in range(4)]
        return lax.psum_scatter(mine, "fsdp", scatter_dimension=0, tiled=True, axis_index_groups=lines)

    def emitter(self):
        whole, left, right = self.order_matrices()
        half = self.wide // 2

        def order(a, pick):
            return dot(a, pick).astype(bf16)

        def begin(name, lhs, rhs):
            if name == "down":
                last = lhs[:, 2 * self.wide :]
                both = jnp.concatenate([order(last, left), order(last, right)], axis=0)
                sides = jnp.concatenate([rhs[:, :half], rhs[:, half:]], axis=0)
                terms = [
                    (lhs[:, : self.wide], rhs),
                    (lhs[:, self.wide : 2 * self.wide], rhs),
                    (both, sides),
                ]
                return self.reduced(terms)
            if name == "gate_up":
                return self.reduced([(lhs, rhs)])
            normed, attended = lhs
            grad_qkv, middle_low, gain_one, gain_two = rhs
            gains = dot_tn(whole, jnp.stack([gain_one, gain_two], axis=1).astype(bf16))
            spare = jnp.zeros((self.wide, self.cols_qkv - self.wide_qkv - 2), f32)
            return self.reduced(
                [(attended, middle_low), (normed, grad_qkv)],
                jnp.concatenate([gains, spare], axis=1),
            )

        return begin

    def shares(self, sums):
        result = []
        for name in ("down", "gate_up", "attention"):
            zero, one = sums[0][name], sums[1][name]
            keep = jnp.where(self.first, zero, one)
            got = self.swap(jnp.where(self.first, one, zero))
            result.append(
                jnp.stack([jnp.where(self.first, keep, got), jnp.where(self.first, got, keep)]).astype(f32)
            )
        down, gate_up, attention = result
        half = self.wide // 2
        cut = self.padded
        last = down[:, :, 2 * self.wide :]
        last = jnp.concatenate([last[:, : cut // 2], last[:, cut // 2 :]], axis=2)
        down = jnp.concatenate([down[:, :, : self.wide], down[:, :, self.wide : 2 * self.wide], last], axis=1)
        down = self.natural_features(down.reshape(2 * self.down_rows, self.wide))
        gate_up = gate_up[:, : self.rows].reshape(2 * self.rows, -1)
        attention = attention[:, : self.rows].reshape(2 * self.rows, -1)
        out = self.natural_features(attention[:, : self.wide])
        qkv = attention[:, self.wide :]
        wide, narrow = HEADS * HD, KV * HD
        return (
            qkv[:, self.wide_qkv],
            qkv[:, :wide],
            qkv[:, wide : wide + narrow],
            qkv[:, wide + narrow : wide + 2 * narrow],
            out,
            qkv[:, self.wide_qkv + 1],
            self.natural_hidden(gate_up[:, : self.hidden]),
            self.natural_hidden(gate_up[:, self.hidden :]),
            down,
        )

    def natural_features(self, array):
        return dot_nt(array.astype(bf16), self.spread)


class Plain:
    def __init__(self, n, features, hidden):
        self.features, self.wide = features, features
        self.first = lax.axis_index("section") == 0
        self.spread = one_hot(features, jnp.arange(features, dtype=jnp.int32))

    def sources(self, weights):
        names = ("gain_one", "query", "key", "value", "out", "gain_two", "gate", "up", "down")
        both = [lax.all_gather(part, ("section", "fsdp"), axis=0, tiled=True) for part in weights]

        def same(a):
            return a

        layers = []
        for layer in range(2):
            w = {name: a.reshape((2, -1) + a.shape[1:])[layer] for name, a in zip(names, both)}
            w["qkv"] = jnp.concatenate([w["query"], w["key"], w["value"]], axis=1)
            w["gain_one"] = w["gain_one"].astype(f32)
            w["gain_two"] = w["gain_two"].astype(f32)
            w["spread"] = self.spread
            for name in ("order", "order_hidden", "relative", "relative_hidden", "back", "back_hidden"):
                w[name] = same
            layers.append(Arriving({}, None))
            layers[-1].tie = lambda value, name: value
            layers[-1].weights = lambda name, w=w: w
        return layers

    def emitter(self):
        def reduced(a):
            part = lax.psum_scatter(a, "fsdp", scatter_dimension=0, tiled=True)
            return lax.psum(part, "section")

        def begin(name, lhs, rhs):
            if name == "attention":
                normed, attended = lhs
                grad_qkv, middle_low, gain_one, gain_two = rhs
                yield ()
                return (
                    reduced(dot_tn(attended, middle_low)),
                    reduced(dot_tn(normed, grad_qkv)),
                    reduced(gain_one),
                    reduced(gain_two),
                )
            yield ()
            return reduced(dot_tn(lhs, rhs))

        return begin

    def shares(self, sums):
        own = jax.tree.map(lambda a, b: jnp.where(self.first, a, b), sums[0], sums[1])
        out, qkv, gain_one, gain_two = own["attention"]
        wide, narrow = HEADS * HD, KV * HD
        hidden = own["gate_up"].shape[1] // 2
        return (
            gain_one,
            qkv[:, :wide],
            qkv[:, wide : wide + narrow],
            qkv[:, wide + narrow :],
            out,
            gain_two,
            own["gate_up"][:, :hidden],
            own["gate_up"][:, hidden:],
            own["down"],
        )


def on_device(inputs, cotangent, segments, positions, *weights):
    n = lax.axis_size("fsdp")
    features = inputs.shape[-1]
    hidden = weights[6].shape[-1]
    fits = n == 16 and features == 960 and hidden == 2560
    plan = (Halves if fits else Plain)(n, features, hidden)
    section = lax.axis_index("section")
    first = section == 0
    source_zero, source_one = plan.sources([weight[0] for weight in weights])
    spread = plan.spread

    def mine(array):
        return lax.dynamic_index_in_dim(array, section, 0, keepdims=False)

    labels = mine(segments)
    length = labels.shape[0]
    token = jnp.arange(length)
    allowed = (labels[:, None] == labels[None, :]) & (token[:, None] >= token[None, :])
    tables = rope_tables(mine(positions))

    start = dot(mine(inputs), spread)
    middle, weights_zero, kept_zero = forward(start, source_zero, allowed, tables, features)
    end, weights_one, kept_one = forward(middle, source_one, allowed, tables, features)

    grad = split_dot(mine(cotangent), spread)
    flow = Flow(plan.emitter())
    grad_middle = backward(middle, weights_one, tables, features, kept_one, grad, flow)
    grad_start = backward(start, weights_zero, tables, features, kept_zero, grad_middle, flow)
    sums_one, sums_zero = flow.finished()

    def exchanged(zero, one):
        keep = jnp.where(first, zero, one)
        sent = jnp.where(first, one, zero).astype(bf16)
        got = lax.ppermute(sent, "section", [(0, 1), (1, 0)])
        kept = keep.astype(bf16)
        rest = (keep - kept.astype(f32)).astype(bf16)
        kept = dot_nt(kept, spread) + dot_nt(rest, spread)
        got = dot_nt(got, spread)
        return jnp.stack([jnp.where(first, kept, got), jnp.where(first, got, kept)])[None]

    activations = exchanged(middle, end)
    input_grads = exchanged(grad_start, grad_middle)
    shares = plan.shares((sums_zero, sums_one))
    return (activations, input_grads) + tuple(share[None] for share in shares)


def solution(mesh):
    rows = P("section", "fsdp")
    matrix = P("section", "fsdp", None)
    weights = (rows, matrix, matrix, matrix, matrix, rows, matrix, matrix, matrix)
    tokens = P(None, "fsdp", None)
    return jax.shard_map(
        on_device,
        mesh=mesh,
        in_specs=(tokens, tokens, P(None, "fsdp"), P(None, "fsdp")) + weights,
        out_specs=(P("section", None, "fsdp", None), P("section", None, "fsdp", None)) + weights,
        check_vma=False,
    )
```

```python
import jax
import jax.numpy as jnp
from jax import lax
from jax.experimental import pallas as pl
from jax.experimental.pallas import tpu as pltpu
from jax.sharding import PartitionSpec as P

HEADS = 15
KV = 5
HD = 64
GROUP = HEADS // KV

SECTION = "section"
FSDP = "fsdp"
BOTH = (SECTION, FSDP)
QKV, OUT, GATE_UP, DOWN = range(4)

bf16 = jnp.bfloat16
f32 = jnp.float32
epsilon = 1e-05
rope_base = 100000.0


def dot(a, b):
    return jnp.dot(a, b, preferred_element_type=f32)


def dot_tn(a, b):
    return lax.dot_general(a, b, (((0,), (0,)), ((), ())), preferred_element_type=f32)


def dot_nt(a, b):
    return lax.dot_general(a, b, (((1,), (1,)), ((), ())), preferred_element_type=f32)


def one_hot(rows, targets):
    count = targets.shape[0]
    row = lax.broadcasted_iota(jnp.int32, (rows, count), 0)
    return (row == targets[None, :]).astype(bf16)


def split_dot(a, pick):
    high = a.astype(bf16)
    low = (a - high.astype(f32)).astype(bf16)
    return dot(high, pick) + dot(low, pick)


def rope_tables(places):
    half = HD // 2
    frequency = rope_base ** (-jnp.arange(half, dtype=f32) / half)
    angles = places.astype(f32)[:, None] * frequency
    cosine, sine = jnp.cos(angles), jnp.sin(angles)
    return jnp.concatenate([cosine] * 4, axis=1), jnp.concatenate([-sine, sine, -sine, sine], axis=1)


def norm_scale(v, features):
    return lax.rsqrt(jnp.sum(v * v, axis=-1, keepdims=True) / features + epsilon)


def norm_back(v, scale, gain, grad, features):
    gain_grad = jnp.sum(grad * v * scale, axis=0)
    weighted = grad * gain
    mean = jnp.sum(weighted * v, axis=-1, keepdims=True) / features
    return scale * weighted - v * (scale * scale * scale) * mean, gain_grad


ROWS = 128


def turned(block, cosine, sine):
    lane = lax.broadcasted_iota(jnp.int32, block.shape, 1)
    other = jnp.where(lane % HD < HD // 2, pltpu.roll(block, 128 - HD // 2, 1), pltpu.roll(block, HD // 2, 1))
    return block * cosine + other * sine


def fill_bias(bias, row_labels, column_labels):
    length = bias.shape[0]
    query = lax.broadcasted_iota(jnp.int32, (length, length), 0)
    key = lax.broadcasted_iota(jnp.int32, (length, length), 1)
    allowed = (row_labels[...] == column_labels[...]) & (query >= key)
    bias[...] = jnp.where(allowed, 0.0, -1e30)


def members(ref, start, rows, group):
    return jnp.concatenate(
        [ref[rows, (group * GROUP + j) * HD + start : (group * GROUP + j + 1) * HD + start] for j in range(GROUP)], axis=0
    )


def softmax(queries, keys, bias):
    scores = lax.dot_general(queries, keys, (((1,), (1,)), ((), ())), preferred_element_type=f32)
    scores = scores + jnp.concatenate([bias] * GROUP, axis=0)
    shifted = jnp.exp(scores - jnp.max(scores, axis=1, keepdims=True))
    return shifted / jnp.sum(shifted, axis=1, keepdims=True)


def attention_kernel(qkv, cosine, sine, row_labels, column_labels, attended, turned_qk, values, bias):
    length = qkv.shape[0]
    wide = HEADS * HD
    narrow = KV * HD
    fill_bias(bias, row_labels, column_labels)
    lane = lax.broadcasted_iota(jnp.int32, (length, 128), 1)
    for at in range(0, wide + narrow, 128):
        scale = jnp.where(lane + at < wide, HD ** -0.5, 1.0)
        block = turned(qkv[:, at : at + 128], cosine[...], sine[...])
        turned_qk[:, at : at + 128] = (block.astype(bf16).astype(f32) * scale).astype(bf16)
    values[...] = qkv[:, wide + narrow : wide + 2 * narrow].astype(bf16)
    for start in range(0, length, ROWS):
        rows = slice(start, start + ROWS)
        upto = slice(0, start + ROWS)
        heads = []
        for group in range(KV):
            queries = members(turned_qk, 0, rows, group)
            keys = turned_qk[upto, wide + group * HD : wide + (group + 1) * HD]
            probs = softmax(queries, keys, bias[rows, upto]).astype(bf16)
            mixed = jnp.dot(probs, values[upto, group * HD : (group + 1) * HD], preferred_element_type=f32)
            heads += [mixed[j * ROWS : (j + 1) * ROWS] for j in range(GROUP)]
        attended[rows, :] = jnp.concatenate(heads, axis=1).astype(bf16)


def attend(qkv, cosine, sine, labels):
    length = qkv.shape[0]
    wide, narrow = HEADS * HD, KV * HD
    return pl.pallas_call(
        attention_kernel,
        out_shape=[
            jax.ShapeDtypeStruct((length, wide), bf16),
            jax.ShapeDtypeStruct((length, wide + narrow), bf16),
            jax.ShapeDtypeStruct((length, narrow), bf16),
        ],
        scratch_shapes=[pltpu.VMEM((length, length), f32)],
        compiler_params=pltpu.CompilerParams(vmem_limit_bytes=32 * 2**20),
        cost_estimate=pl.CostEstimate(flops=4 * length * length * wide, bytes_accessed=length * 10000, transcendentals=length * length * HEADS),
    )(qkv, cosine, sine, labels[:, None], labels[None, :])


def attention_back_kernel(turned_qk, values, grad_att, cosine, sine, row_labels, column_labels, grad_qkv, bias, grad_q, grad_v):
    length = turned_qk.shape[0]
    wide = HEADS * HD
    narrow = KV * HD
    fill_bias(bias, row_labels, column_labels)
    contract = (((0,), (0,)), ((), ()))
    for group in range(KV):
        total_k = [None] * (length // ROWS)
        total_v = [None] * (length // ROWS)
        for start in range(0, length, ROWS):
            rows = slice(start, start + ROWS)
            upto = slice(0, start + ROWS)
            queries = members(turned_qk, 0, rows, group)
            keys = turned_qk[upto, wide + group * HD : wide + (group + 1) * HD]
            mixed = values[upto, group * HD : (group + 1) * HD]
            grads = members(grad_att, 0, rows, group)
            probs = softmax(queries, keys, bias[rows, upto])
            grad_probs = lax.dot_general(grads, mixed, (((1,), (1,)), ((), ())), preferred_element_type=f32)
            part_v = lax.dot_general(probs.astype(bf16), grads, contract, preferred_element_type=f32)
            low = (probs * (grad_probs - jnp.sum(probs * grad_probs, axis=1, keepdims=True))).astype(bf16)
            part_k = lax.dot_general(low, queries, contract, preferred_element_type=f32)
            turned_back = jnp.dot(low, keys, preferred_element_type=f32) * HD ** -0.5
            for j in range(GROUP):
                head = group * GROUP + j
                grad_q[rows, head * HD : (head + 1) * HD] = turned_back[j * ROWS : (j + 1) * ROWS]
            for piece in range(start // ROWS + 1):
                inside = slice(piece * ROWS, (piece + 1) * ROWS)
                total_k[piece] = part_k[inside] if total_k[piece] is None else total_k[piece] + part_k[inside]
                total_v[piece] = part_v[inside] if total_v[piece] is None else total_v[piece] + part_v[inside]
        for piece in range(length // ROWS):
            inside = slice(piece * ROWS, (piece + 1) * ROWS)
            grad_q[inside, wide + group * HD : wide + (group + 1) * HD] = total_k[piece]
            grad_v[inside, group * HD : (group + 1) * HD] = total_v[piece]
    for at in range(0, wide + narrow, 128):
        grad_qkv[:, at : at + 128] = turned(grad_q[:, at : at + 128], cosine[...], -sine[...]).astype(bf16)
    grad_qkv[:, wide + narrow : wide + 2 * narrow] = grad_v[...].astype(bf16)


def attend_back(turned_qk, values, grad_att, cosine, sine, labels):
    length = turned_qk.shape[0]
    wide, narrow = HEADS * HD, KV * HD
    return pl.pallas_call(
        attention_back_kernel,
        out_shape=jax.ShapeDtypeStruct((length, wide + 2 * narrow), bf16),
        scratch_shapes=[pltpu.VMEM((length, length), f32), pltpu.VMEM((length, wide + narrow), f32), pltpu.VMEM((length, narrow), f32)],
        compiler_params=pltpu.CompilerParams(vmem_limit_bytes=32 * 2**20),
        cost_estimate=pl.CostEstimate(flops=10 * length * length * wide, bytes_accessed=length * 10000, transcendentals=length * length * HEADS),
    )(turned_qk, values, grad_att, cosine, sine, labels[:, None], labels[None, :])


def forward(x, source, layer, labels, tables, features):
    turn = iter(source.order[layer])
    x = source.tie(x, next(turn))
    w = source.weights(layer)
    scale_one = norm_scale(x, features)
    normed = (x * scale_one * w.gain_one).astype(bf16)
    qkv = dot(normed, w.qkv)
    qkv = source.tie(qkv, next(turn))
    attended, turned_qk, values = attend(qkv, *tables, labels)
    attended = dot(attended, w.spread).astype(bf16)
    attended = source.tie(attended, next(turn))
    middle = x + dot(attended, w.out)
    middle = source.tie(middle, next(turn))
    w = source.weights(layer)
    scale_two = norm_scale(middle, features)
    second = (middle * scale_two * w.gain_two).astype(bf16)
    gate = dot(second, w.gate)
    up = dot(second, w.up)
    hidden = (jax.nn.silu(gate) * up).astype(bf16)
    hidden = source.tie(hidden, next(turn))
    w = source.weights(layer)
    output = middle + dot(hidden, w.down)
    return output, w, (
        scale_one, normed, turned_qk, values, attended, middle, scale_two, second, gate, up, hidden,
    )


def backward(x, w, labels, tables, features, kept, grad, flow):
    (scale_one, normed, turned_qk, values, attended, middle, scale_two, second, gate, up, hidden) = kept
    low = grad.astype(bf16)
    flow.begin(DOWN, hidden, low)
    grad_hidden = dot_nt(low, w.down)
    sig = jax.nn.sigmoid(gate)
    silu = gate * sig
    gate_low = (grad_hidden * up * (sig * (1.0 + gate * (1.0 - sig)))).astype(bf16)
    up_low = (grad_hidden * silu).astype(bf16)
    gate_low, up_low = flow.tie((gate_low, up_low), (DOWN,), (QKV, OUT))
    flow.begin(GATE_UP, second, jnp.concatenate([gate_low, up_low], axis=1))
    grad_second = dot_nt(gate_low, w.gate) + dot_nt(up_low, w.up)
    grad_norm, gain_two = norm_back(middle, scale_two, w.gain_two, grad_second, features)
    grad_middle = grad + grad_norm
    grad_middle = flow.tie(grad_middle, (GATE_UP,), (QKV, OUT))
    middle_low = grad_middle.astype(bf16)
    flow.begin(OUT, attended, middle_low)
    grad_att = dot_nt(middle_low, w.out).astype(bf16)
    grad_att = dot_nt(grad_att, w.spread).astype(bf16)
    grad_att = flow.tie(grad_att, (DOWN, OUT), ())
    grad_qkv = attend_back(turned_qk, values, grad_att, *tables, labels)
    grad_qkv = flow.tie(grad_qkv, (DOWN, GATE_UP), (DOWN, QKV))
    grad_normed = dot_nt(grad_qkv, w.qkv)
    grad_norm, gain_one = norm_back(x, scale_one, w.gain_one, grad_normed, features)
    flow.begin(QKV, normed, (grad_qkv, gain_one, gain_two))
    grad = flow.tie(grad_middle + grad_norm, (QKV, GATE_UP, OUT), (GATE_UP,))
    flow.next_layer()
    return grad


class Weights:
    def __init__(self, **fields):
        self.__dict__.update(fields)


class Arriving:
    order = (
        ((0, 1, 0, 2, 0, 1, 0, 3, 1, 2, 0), (2, 3), (4, 1), (1, 3), (4, 5, 2, 2)),
        ((4, 3, 3), (5,), (5, 4), (4,), (5, 5)),
    )

    def __init__(self, groups, unpack):
        self.groups = [(steps, next(steps)) for steps in groups]
        self.unpack = unpack

    def tie(self, value, turns):
        for index in turns:
            steps, waited = self.groups[index]
            value, got = lax.optimization_barrier((value, waited))
            try:
                self.groups[index] = (steps, steps.send(got))
            except StopIteration as end:
                self.groups[index] = (None, end.value)
        return value

    def weights(self, layer):
        return self.unpack([got for steps, got in self.groups[3 * layer : 3 * layer + 3] if steps is None])


class Flow:
    def __init__(self, begin):
        self.begun = begin
        self.now, self.before, self.done = {}, {}, []

    def begin(self, name, lhs, rhs):
        steps = self.begun(name, lhs, rhs)
        self.now[name] = (steps, next(steps))

    def tie(self, value, now, before):
        tables = [(self.now, n) for n in now] + [(self.before, n) for n in before]
        tables = [(table, n) for table, n in tables if n in table and table[n][0] is not None]
        value, waited = lax.optimization_barrier((value, [table[n][1] for table, n in tables]))
        for (table, n), got in zip(tables, waited):
            self.advance(table, n, got)
        return value

    def advance(self, table, name, got):
        steps = table[name][0]
        try:
            table[name] = (steps, steps.send(got))
        except StopIteration as end:
            table[name] = (None, end.value)

    def next_layer(self):
        self.done.append(self.before)
        self.before, self.now = self.now, {}

    def finished(self):
        last, earlier = self.before, self.done[1:]
        self.tie((), (), (QKV, OUT))
        others = [table[name] for table in earlier for name in table] + [last[DOWN]]
        waited = self.tie([got for steps, got in others], (), (QKV,))
        for table in earlier:
            for name in table:
                table[name] = (table[name][0], waited.pop(0))
        last[DOWN] = (last[DOWN][0], waited.pop(0))
        self.tie((), (), (QKV, OUT, GATE_UP))
        for table in earlier + [last]:
            while any(steps is not None for steps, _ in table.values()):
                for name in table:
                    if table[name][0] is not None:
                        self.advance(table, name, table[name][1])
        return [{name: value for name, (_, value) in table.items()} for table in earlier + [last]]


class Halves:
    def __init__(self, n, features, hidden):
        self.n, self.features, self.hidden = n, features, hidden
        self.parts = 2 * n
        self.rows = features // self.parts
        self.padded = -(-self.rows // 16) * 16
        self.wide = self.parts * self.padded
        self.down_rows = hidden // self.parts
        self.section = lax.axis_index(SECTION)
        self.first = self.section == 0
        self.place = lax.axis_index(FSDP)
        lane = jnp.arange(self.wide, dtype=jnp.int32)
        inside = lane % self.padded
        natural = jnp.where(inside < self.rows, lane // self.padded * self.rows + inside, -1)
        self.spread = one_hot(features, natural)
        self.y = self.place // 2 % 2
        self.x = self.place % 2
        z, depth = self.place // 4, n // 4
        self.relative = self.block_order(lambda m: m)
        self.arrival = self.block_order(lambda m: (z - m + depth) % depth)

    def permuted_hidden(self, array):
        rows = array.shape[0]
        blocks = array.reshape(rows, self.parts, self.down_rows)
        cut = self.padded
        return jnp.concatenate(
            [
                blocks[:, :, :cut].reshape(rows, -1),
                blocks[:, :, cut : 2 * cut].reshape(rows, -1),
                blocks[:, :, 2 * cut :].reshape(rows, -1),
            ],
            axis=1,
        )

    def natural_hidden(self, array):
        rows = array.shape[0]
        cut = self.padded
        third = self.down_rows - 2 * cut
        one = array[:, : self.wide].reshape(rows, self.parts, cut)
        two = array[:, self.wide : 2 * self.wide].reshape(rows, self.parts, cut)
        three = array[:, 2 * self.wide :].reshape(rows, self.parts, third)
        return jnp.concatenate([one, two, three], axis=2).reshape(rows, self.hidden)

    def swap(self, array):
        return lax.ppermute(array, SECTION, [(0, 1), (1, 0)])

    def packed(self, weights):
        gain_one, query, key, value, out, gain_two, gate, up, down = weights
        self.wide_qkv = query.shape[1] + key.shape[1] + value.shape[1]
        self.cols_qkv = -(-(self.wide_qkv + 2) // 128) * 128
        spare = self.cols_qkv - self.wide_qkv - 2
        rows = query.shape[0]
        half = self.wide // 2

        def halves(parts):
            both = jnp.concatenate(parts, axis=1).reshape(2, self.rows, -1)
            return jnp.pad(both, ((0, 0), (0, self.padded - self.rows), (0, 0)))

        cut = self.padded
        carried = [self.carried(halves([
            query, key, value, gain_one[:, None], gain_two[:, None], jnp.zeros((rows, spare), bf16),
            dot(out, self.spread).astype(bf16),
        ]))]
        (gate, up, down), carried = lax.optimization_barrier(((gate, up, down), carried))
        carried.append(self.carried(halves([self.permuted_hidden(gate), self.permuted_hidden(up)])))
        down = dot(down, self.spread).astype(bf16).reshape(2, self.down_rows, self.wide)
        last = down[:, 2 * cut :]
        last = jnp.concatenate([last[:, :, :half], last[:, :, half:]], axis=1)
        carried.append(self.carried(jnp.concatenate([down[:, :cut], down[:, cut : 2 * cut], last], axis=2)))
        return [zero for zero, one in carried] + [one for zero, one in carried]

    def carried(self, halves):
        keep = jnp.where(self.first, halves[0], halves[1])
        got = self.swap(jnp.where(self.first, halves[1], halves[0]))
        return jnp.where(self.first, keep, got), jnp.where(self.first, got, keep)

    def source(self, weights):
        groups = [self.travelled(part) for part in self.packed(weights)]
        self.whole, self.left, self.right = self.order_matrices()

        def unpack(groups):
            w = Weights(spread=self.spread)
            for unpacked, pieces in zip((self.attention, self.gate_up, self.down), groups):
                unpacked(w, pieces)
            return w

        return Arriving(groups, unpack)

    def assembled(self, pieces, shape, places):
        depth = self.n // 4
        part = self.padded
        count = len(places)

        def kernel(index, *refs):
            sources, out, held, came, gone = refs[: len(pieces)], *refs[len(pieces) :]
            arriving, leaving = [], []
            for number, source in enumerate(sources):
                arriving.append(pltpu.make_async_copy(source, held.at[number], came.at[number]))
                for m in range(depth):
                    block = number * depth + m
                    for place, (rows, columns, base, step, column) in enumerate(places):
                        leaving.append(
                            pltpu.make_async_copy(
                                held.at[
                                    number, pl.ds(m * part + rows[0], rows[1]), pl.ds(columns[0], columns[1])
                                ],
                                out.at[
                                    pl.ds(pl.multiple_of(base + index[block] * step, 16), rows[1]),
                                    pl.ds(column, columns[1]),
                                ],
                                gone.at[block * count + place],
                            )
                        )
            for copy in arriving:
                copy.start()
            for number, copy in enumerate(arriving):
                copy.wait()
                for sent in leaving[number * depth * count : (number + 1) * depth * count]:
                    sent.start()
            for copy in leaving:
                copy.wait()

        anywhere = pl.BlockSpec(memory_space=pl.ANY)
        return pl.pallas_call(
            kernel,
            out_shape=jax.ShapeDtypeStruct(shape, bf16),
            in_specs=[pl.BlockSpec(memory_space=pltpu.SMEM)] + [anywhere] * len(pieces),
            out_specs=anywhere,
            scratch_shapes=[
                pltpu.VMEM((len(pieces),) + pieces[0].shape, bf16),
                pltpu.SemaphoreType.DMA((len(pieces),)),
                pltpu.SemaphoreType.DMA((self.parts * count,)),
            ],
            compiler_params=pltpu.CompilerParams(vmem_limit_bytes=16 * 2**20),
            cost_estimate=pl.CostEstimate(
                flops=0, bytes_accessed=4 * shape[0] * shape[1], transcendentals=0
            ),
        )(self.arrival, *pieces)

    def side_by_side(self, pieces):
        columns = pieces[0].shape[1]
        rows = self.padded
        return self.assembled(pieces, (self.wide, columns), [((0, rows), (0, columns), 0, rows, 0)])

    def attention(self, w, pieces):
        group = self.side_by_side(pieces)
        gains = group[:, self.wide_qkv : self.wide_qkv + 2].astype(f32).T
        w.gain_one, w.gain_two = gains[0], gains[1]
        w.qkv, w.out = group[:, : self.wide_qkv], group[:, self.cols_qkv :]

    def gate_up(self, w, pieces):
        group = self.side_by_side(pieces)
        w.gate, w.up = group[:, : self.hidden], group[:, self.hidden :]

    def down(self, w, pieces):
        wide, cut = self.wide, self.padded
        short, half = cut // 2, wide // 2
        w.down = self.assembled(
            pieces,
            (self.hidden, wide),
            [
                ((0, cut), (0, wide), 0, cut, 0),
                ((0, cut), (wide, wide), wide, cut, 0),
                ((0, short), (2 * wide, half), 2 * wide, short, 0),
                ((short, short), (2 * wide, half), 2 * wide, short, half),
            ],
        )

    def travelled(self, part):
        depth = self.n // 4
        part = yield part
        got = yield [
            lax.ppermute(part, FSDP, [(i, (i + 4 * k) % self.n) for i in range(self.n)])
            for k in range(1, depth)
        ]
        line = jnp.concatenate([part] + list(got), axis=0)
        first_route, second_route = self.routes()
        far = lax.ppermute(line, BOTH, first_route)
        across = [self.swap(line)]
        got = yield lax.ppermute(line, BOTH, second_route)
        across.append(self.swap(got))
        mine = [line, got]
        got = yield [far, lax.ppermute(got, BOTH, first_route)]
        across += [self.swap(one) for one in got]
        mine += got
        across = yield across
        return mine + across

    def block_order(self, chip_z):
        depth = self.n // 4
        block = jnp.arange(self.parts, dtype=jnp.int32)
        quarter = block // depth % 4
        core = self.section ^ (block // self.n)
        low, high = quarter % 2, quarter // 2
        other_x = jnp.where(core == 0, low, high)
        other_y = jnp.where(core == 0, high, low)
        chip = chip_z(block % depth) * 4 + (self.y ^ other_y) * 2 + (self.x ^ other_x)
        return chip * 2 + core

    def order_matrices(self):
        lane = jnp.arange(self.wide, dtype=jnp.int32)
        part = jnp.repeat(self.relative, self.padded)
        inside = lane % self.padded
        half = self.padded // 2
        block = part * half
        return (
            one_hot(self.wide, part * self.padded + inside),
            one_hot(self.wide // 2, jnp.where(inside < half, block + inside, -1)),
            one_hot(self.wide // 2, jnp.where(inside >= half, block + inside - half, -1)),
        )

    def routes(self):
        count = self.n

        def route(flips):
            return [
                (core * count + i, core * count + (i ^ flip))
                for core, flip in enumerate(flips)
                for i in range(count)
            ]

        return route((2, 1)), route((1, 2))

    def reduced(self, terms, direct=False):
        half = self.wide // 2

        def product(lo, hi):
            return jnp.concatenate([dot_tn(a[:, lo:hi], b) for a, b in terms], axis=1)

        first_route, second_route = self.routes()
        got = yield self.swap(product(half, self.wide).astype(bf16))
        mine = (product(0, half) + got.astype(f32)).astype(bf16)
        got = yield lax.ppermute(mine[half // 2 :], BOTH, first_route)
        mine = (mine[: half // 2].astype(f32) + got.astype(f32)).astype(bf16)
        got = yield lax.ppermute(mine[half // 4 :], BOTH, second_route)
        mine = (mine[: half // 4].astype(f32) + got.astype(f32)).astype(bf16)
        depth, part = self.n // 4, self.padded
        if direct:
            blocks = [
                lax.dynamic_slice_in_dim(mine, (self.place // 4 + k) % depth * part, part, 0)
                for k in range(depth)
            ]
            got = yield [
                lax.ppermute(blocks[k], FSDP, [(i, (i + 4 * k) % self.n) for i in range(self.n)])
                for k in range(1, depth)
            ]
            return sum((one.astype(f32) for one in got), blocks[0].astype(f32)).astype(bf16)
        lines = [[q + 4 * z for z in range(depth)] for q in range(4)]
        got = yield lax.psum_scatter(mine, FSDP, scatter_dimension=0, tiled=True, axis_index_groups=lines)
        return got

    def emitter(self):
        whole, half = self.whole, self.wide // 2

        def order(a):
            return dot(a, whole).astype(bf16)

        def begin(name, lhs, rhs):
            if name == DOWN:
                last = lhs[:, 2 * self.wide :]
                both = jnp.concatenate(
                    [dot(last, self.left).astype(bf16), dot(last, self.right).astype(bf16)], axis=0
                )
                sides = jnp.concatenate([rhs[:, :half], rhs[:, half:]], axis=0)
                terms = [
                    (order(lhs[:, : self.wide]), rhs),
                    (order(lhs[:, self.wide : 2 * self.wide]), rhs),
                    (both, sides),
                ]
                return self.reduced(terms)
            if name == GATE_UP:
                return self.reduced([(order(lhs), rhs)])
            if name == OUT:
                return self.reduced([(order(lhs), rhs)], direct=True)
            grad_qkv, gain_one, gain_two = rhs
            length = lhs.shape[0]
            gains = jnp.pad(jnp.stack([gain_one, gain_two]), ((0, 14), (0, 0))).astype(bf16)
            ones = (jnp.arange(16)[:, None] == jnp.arange(self.cols_qkv)[None, :] - self.wide_qkv).astype(bf16)
            rhs = jnp.pad(grad_qkv, ((0, 0), (0, self.cols_qkv - self.wide_qkv)))
            rhs = jnp.concatenate([rhs, ones], axis=0)
            return self.reduced([(order(jnp.concatenate([lhs, gains], axis=0)), rhs)], direct=True)

        return begin

    def shares(self, sums):
        result = []
        for name in (DOWN, GATE_UP, OUT, QKV):
            zero, one = sums[0][name], sums[1][name]
            keep = jnp.where(self.first, zero, one)
            got = self.swap(jnp.where(self.first, one, zero))
            result.append(
                jnp.stack([jnp.where(self.first, keep, got), jnp.where(self.first, got, keep)]).astype(f32)
            )
        down, gate_up, out, qkv = result
        half = self.wide // 2
        cut = self.padded
        last = down[:, :, 2 * self.wide :]
        last = jnp.concatenate([last[:, : cut // 2], last[:, cut // 2 :]], axis=2)
        down = jnp.concatenate([down[:, :, : self.wide], down[:, :, self.wide : 2 * self.wide], last], axis=1)
        down = self.natural_features(down.reshape(2 * self.down_rows, self.wide))
        gate_up = gate_up[:, : self.rows].reshape(2 * self.rows, -1)
        out = self.natural_features(out[:, : self.rows].reshape(2 * self.rows, -1))
        qkv = qkv[:, : self.rows].reshape(2 * self.rows, -1)
        wide, narrow = HEADS * HD, KV * HD
        return (
            qkv[:, self.wide_qkv],
            qkv[:, :wide],
            qkv[:, wide : wide + narrow],
            qkv[:, wide + narrow : wide + 2 * narrow],
            out,
            qkv[:, self.wide_qkv + 1],
            self.natural_hidden(gate_up[:, : self.hidden]),
            self.natural_hidden(gate_up[:, self.hidden :]),
            down,
        )

    def natural_features(self, array):
        return dot_nt(array.astype(bf16), self.spread)


class Plain:
    def __init__(self, n, features, hidden):
        self.first = lax.axis_index(SECTION) == 0
        self.spread = one_hot(features, jnp.arange(features, dtype=jnp.int32))

    def source(self, weights):
        both = [lax.all_gather(part, (SECTION, FSDP), axis=0, tiled=True) for part in weights]
        both = [a.reshape((2, -1) + a.shape[1:]) for a in both]

        def layer_of(layer):
            gain_one, query, key, value, out, gain_two, gate, up, down = [a[layer] for a in both]
            return Weights(
                gain_one=gain_one.astype(f32), gain_two=gain_two.astype(f32), out=out, gate=gate, up=up,
                down=down, qkv=jnp.concatenate([query, key, value], axis=1), spread=self.spread,
            )

        source = Arriving([], None)
        source.tie = lambda value, turns: value
        source.weights = layer_of
        return source

    def emitter(self):
        def reduced(a):
            part = lax.psum_scatter(a, FSDP, scatter_dimension=0, tiled=True)
            return lax.psum(part, SECTION)

        def begin(name, lhs, rhs):
            if name == QKV:
                grad_qkv, gain_one, gain_two = rhs
                yield ()
                return reduced(dot_tn(lhs, grad_qkv)), reduced(gain_one), reduced(gain_two)
            yield ()
            return reduced(dot_tn(lhs, rhs))

        return begin

    def shares(self, sums):
        own = jax.tree.map(lambda a, b: jnp.where(self.first, a, b), sums[0], sums[1])
        qkv, gain_one, gain_two = own[QKV]
        wide, narrow = HEADS * HD, KV * HD
        both = own[GATE_UP]
        hidden = both.shape[1] // 2
        return (
            gain_one,
            qkv[:, :wide],
            qkv[:, wide : wide + narrow],
            qkv[:, wide + narrow :],
            own[OUT],
            gain_two,
            both[:, :hidden],
            both[:, hidden:],
            own[DOWN],
        )


def on_device(inputs, cotangent, segments, positions, *weights):
    n = lax.axis_size(FSDP)
    features = inputs.shape[-1]
    hidden = weights[6].shape[-1]
    fits = n == 16 and features == 960 and hidden == 2560
    plan = (Halves if fits else Plain)(n, features, hidden)
    section = lax.axis_index(SECTION)
    first = section == 0
    source = plan.source([weight[0] for weight in weights])
    spread = plan.spread

    def mine(array):
        return lax.dynamic_index_in_dim(array, section, 0, keepdims=False)

    labels = mine(segments)
    tables = rope_tables(mine(positions))

    start = dot(mine(inputs), spread)
    middle, weights_zero, kept_zero = forward(start, source, 0, labels, tables, features)
    end, weights_one, kept_one = forward(middle, source, 1, labels, tables, features)

    grad = split_dot(mine(cotangent), spread)
    flow = Flow(plan.emitter())
    grad_middle = backward(middle, weights_one, labels, tables, features, kept_one, grad, flow)
    grad_start = backward(start, weights_zero, labels, tables, features, kept_zero, grad_middle, flow)
    sums_one, sums_zero = flow.finished()

    def exchanged(zero, one):
        keep = jnp.where(first, zero, one)
        sent = jnp.where(first, one, zero).astype(bf16)
        got = lax.ppermute(sent, SECTION, [(0, 1), (1, 0)])
        kept = keep.astype(bf16)
        rest = (keep - kept.astype(f32)).astype(bf16)
        kept = dot_nt(kept, spread) + dot_nt(rest, spread)
        got = dot_nt(got, spread)
        return jnp.stack([jnp.where(first, kept, got), jnp.where(first, got, kept)])[None]

    activations = exchanged(middle, end)
    input_grads = exchanged(grad_start, grad_middle)
    shares = plan.shares((sums_zero, sums_one))
    return (activations, input_grads) + tuple(share[None] for share in shares)


def solution(mesh):
    rows = P(SECTION, FSDP)
    matrix = P(SECTION, FSDP, None)
    weights = (rows, matrix, matrix, matrix, matrix, rows, matrix, matrix, matrix)
    tokens = P(None, FSDP, None)
    return jax.shard_map(
        on_device,
        mesh=mesh,
        in_specs=(tokens, tokens, P(None, FSDP), P(None, FSDP)) + weights,
        out_specs=(P(SECTION, None, FSDP, None), P(SECTION, None, FSDP, None)) + weights,
        check_vma=False,
    )
```

```python
import jax
import jax.numpy as jnp
from jax import lax
from jax.experimental import pallas as pl
from jax.experimental.pallas import tpu as pltpu
from jax.sharding import PartitionSpec as P

HEADS = 15
KV = 5
HD = 64
GROUP = HEADS // KV

SECTION = "section"
FSDP = "fsdp"
BOTH = (SECTION, FSDP)
QKV, OUT, GATE_UP, DOWN = range(4)

bf16 = jnp.bfloat16
f32 = jnp.float32
epsilon = 1e-05
rope_base = 100000.0


def dot(a, b):
    return jnp.dot(a, b, preferred_element_type=f32)


def dot_tn(a, b):
    return lax.dot_general(a, b, (((0,), (0,)), ((), ())), preferred_element_type=f32)


def dot_nt(a, b):
    return lax.dot_general(a, b, (((1,), (1,)), ((), ())), preferred_element_type=f32)


def one_hot(rows, targets):
    count = targets.shape[0]
    row = lax.broadcasted_iota(jnp.int32, (rows, count), 0)
    return (row == targets[None, :]).astype(bf16)


def split_dot(a, pick):
    high = a.astype(bf16)
    low = (a - high.astype(f32)).astype(bf16)
    return dot(high, pick) + dot(low, pick)


def rope_tables(places):
    half = HD // 2
    frequency = rope_base ** (-jnp.arange(half, dtype=f32) / half)
    angles = places.astype(f32)[:, None] * frequency
    cosine, sine = jnp.cos(angles), jnp.sin(angles)
    return jnp.concatenate([cosine] * 4, axis=1), jnp.concatenate([-sine, sine, -sine, sine], axis=1)


def norm_scale(v, features):
    return lax.rsqrt(jnp.sum(v * v, axis=-1, keepdims=True) / features + epsilon)


def norm_back(v, scale, gain, grad, features):
    gain_grad = jnp.sum(grad * v * scale, axis=0)
    weighted = grad * gain
    mean = jnp.sum(weighted * v, axis=-1, keepdims=True) / features
    return scale * weighted - v * (scale * scale * scale) * mean, gain_grad


ROWS = 128


def turned(block, cosine, sine):
    lane = lax.broadcasted_iota(jnp.int32, block.shape, 1)
    other = jnp.where(lane % HD < HD // 2, pltpu.roll(block, 128 - HD // 2, 1), pltpu.roll(block, HD // 2, 1))
    return block * cosine + other * sine


def fill_bias(bias, row_labels, column_labels):
    length = bias.shape[0]
    query = lax.broadcasted_iota(jnp.int32, (length, length), 0)
    key = lax.broadcasted_iota(jnp.int32, (length, length), 1)
    allowed = (row_labels[...] == column_labels[...]) & (query >= key)
    bias[...] = jnp.where(allowed, 0.0, -1e30)


def members(ref, start, rows, group):
    return jnp.concatenate(
        [ref[rows, (group * GROUP + j) * HD + start : (group * GROUP + j + 1) * HD + start] for j in range(GROUP)], axis=0
    )


def softmax(queries, keys, bias):
    scores = lax.dot_general(queries, keys, (((1,), (1,)), ((), ())), preferred_element_type=f32)
    scores = scores + jnp.concatenate([bias] * GROUP, axis=0)
    shifted = jnp.exp(scores - jnp.max(scores, axis=1, keepdims=True))
    return shifted / jnp.sum(shifted, axis=1, keepdims=True)


def attention_kernel(qkv, cosine, sine, row_labels, column_labels, attended, turned_qk, values, bias):
    length = qkv.shape[0]
    wide = HEADS * HD
    narrow = KV * HD
    fill_bias(bias, row_labels, column_labels)
    lane = lax.broadcasted_iota(jnp.int32, (length, 128), 1)
    for at in range(0, wide + narrow, 128):
        scale = jnp.where(lane + at < wide, HD ** -0.5, 1.0)
        block = turned(qkv[:, at : at + 128], cosine[...], sine[...])
        turned_qk[:, at : at + 128] = (block.astype(bf16).astype(f32) * scale).astype(bf16)
    values[...] = qkv[:, wide + narrow : wide + 2 * narrow].astype(bf16)
    for start in range(0, length, ROWS):
        rows = slice(start, start + ROWS)
        upto = slice(0, start + ROWS)
        heads = []
        for group in range(KV):
            queries = members(turned_qk, 0, rows, group)
            keys = turned_qk[upto, wide + group * HD : wide + (group + 1) * HD]
            probs = softmax(queries, keys, bias[rows, upto]).astype(bf16)
            mixed = jnp.dot(probs, values[upto, group * HD : (group + 1) * HD], preferred_element_type=f32)
            heads += [mixed[j * ROWS : (j + 1) * ROWS] for j in range(GROUP)]
        attended[rows, :] = jnp.concatenate(heads, axis=1).astype(bf16)


def attend(qkv, cosine, sine, labels):
    length = qkv.shape[0]
    wide, narrow = HEADS * HD, KV * HD
    return pl.pallas_call(
        attention_kernel,
        out_shape=[
            jax.ShapeDtypeStruct((length, wide), bf16),
            jax.ShapeDtypeStruct((length, wide + narrow), bf16),
            jax.ShapeDtypeStruct((length, narrow), bf16),
        ],
        scratch_shapes=[pltpu.VMEM((length, length), f32)],
        compiler_params=pltpu.CompilerParams(vmem_limit_bytes=32 * 2**20),
        cost_estimate=pl.CostEstimate(flops=0, bytes_accessed=0, transcendentals=0),
    )(qkv, cosine, sine, labels[:, None], labels[None, :])


def attention_back_kernel(turned_qk, values, grad_att, cosine, sine, row_labels, column_labels, grad_qkv, bias, grad_q, grad_v):
    length = turned_qk.shape[0]
    wide = HEADS * HD
    narrow = KV * HD
    fill_bias(bias, row_labels, column_labels)
    contract = (((0,), (0,)), ((), ()))
    for group in range(KV):
        total_k = [None] * (length // ROWS)
        total_v = [None] * (length // ROWS)
        for start in range(0, length, ROWS):
            rows = slice(start, start + ROWS)
            upto = slice(0, start + ROWS)
            queries = members(turned_qk, 0, rows, group)
            keys = turned_qk[upto, wide + group * HD : wide + (group + 1) * HD]
            mixed = values[upto, group * HD : (group + 1) * HD]
            grads = members(grad_att, 0, rows, group)
            probs = softmax(queries, keys, bias[rows, upto])
            grad_probs = lax.dot_general(grads, mixed, (((1,), (1,)), ((), ())), preferred_element_type=f32)
            part_v = lax.dot_general(probs.astype(bf16), grads, contract, preferred_element_type=f32)
            low = (probs * (grad_probs - jnp.sum(probs * grad_probs, axis=1, keepdims=True))).astype(bf16)
            part_k = lax.dot_general(low, queries, contract, preferred_element_type=f32)
            turned_back = jnp.dot(low, keys, preferred_element_type=f32) * HD ** -0.5
            for j in range(GROUP):
                head = group * GROUP + j
                grad_q[rows, head * HD : (head + 1) * HD] = turned_back[j * ROWS : (j + 1) * ROWS]
            for piece in range(start // ROWS + 1):
                inside = slice(piece * ROWS, (piece + 1) * ROWS)
                total_k[piece] = part_k[inside] if total_k[piece] is None else total_k[piece] + part_k[inside]
                total_v[piece] = part_v[inside] if total_v[piece] is None else total_v[piece] + part_v[inside]
        for piece in range(length // ROWS):
            inside = slice(piece * ROWS, (piece + 1) * ROWS)
            grad_q[inside, wide + group * HD : wide + (group + 1) * HD] = total_k[piece]
            grad_v[inside, group * HD : (group + 1) * HD] = total_v[piece]
    for at in range(0, wide + narrow, 128):
        grad_qkv[:, at : at + 128] = turned(grad_q[:, at : at + 128], cosine[...], -sine[...]).astype(bf16)
    grad_qkv[:, wide + narrow : wide + 2 * narrow] = grad_v[...].astype(bf16)


def attend_back(turned_qk, values, grad_att, cosine, sine, labels):
    length = turned_qk.shape[0]
    wide, narrow = HEADS * HD, KV * HD
    return pl.pallas_call(
        attention_back_kernel,
        out_shape=jax.ShapeDtypeStruct((length, wide + 2 * narrow), bf16),
        scratch_shapes=[pltpu.VMEM((length, length), f32), pltpu.VMEM((length, wide + narrow), f32), pltpu.VMEM((length, narrow), f32)],
        compiler_params=pltpu.CompilerParams(vmem_limit_bytes=32 * 2**20),
        cost_estimate=pl.CostEstimate(flops=0, bytes_accessed=0, transcendentals=0),
    )(turned_qk, values, grad_att, cosine, sine, labels[:, None], labels[None, :])


def forward(x, source, layer, labels, tables, features, early=None):
    turn = iter(source.order[layer])
    x = source.tie(x, next(turn))
    w = source.weights(layer)
    scale_one = norm_scale(x, features)
    normed = (x * scale_one * w.gain_one).astype(bf16)
    qkv = dot(normed, w.qkv)
    qkv = source.tie(qkv, next(turn))
    attended, turned_qk, values = attend(qkv, *tables, labels)
    attended = dot(attended, w.spread).astype(bf16)
    attended = source.tie(attended, next(turn))
    middle = x + dot(attended, w.out)
    middle = source.tie(middle, next(turn))
    w = source.weights(layer)
    scale_two = norm_scale(middle, features)
    second = (middle * scale_two * w.gain_two).astype(bf16)
    gate = dot(second, w.gate)
    up = dot(second, w.up)
    hidden = (jax.nn.silu(gate) * up).astype(bf16)
    hidden = source.tie(hidden, next(turn))
    if early is not None:
        early.begin(DOWN, w.order_hidden(hidden), early.low)
    hidden = source.tie(hidden, next(turn))
    w = source.weights(layer)
    output = middle + dot(hidden, w.down)
    ordered = w.order(normed), w.order(attended), w.order(second), w.order_hidden(hidden)
    if early is None:
        output, ordered = lax.optimization_barrier((output, ordered))
    return output, w, (scale_one, turned_qk, values, middle, scale_two, gate, up, ordered)


def backward(x, w, labels, tables, features, kept, grad, flow):
    scale_one, turned_qk, values, middle, scale_two, gate, up, ordered = kept
    normed, attended, second, hidden = ordered
    low = grad.astype(bf16)
    early = DOWN in flow.now
    if early:
        low = flow.tie(low, (DOWN,), ())
    else:
        flow.begin(DOWN, hidden, low)
    grad_hidden = dot_nt(low, w.down)
    sig = jax.nn.sigmoid(gate)
    silu = gate * sig
    gate_low = (grad_hidden * up * (sig * (1.0 + gate * (1.0 - sig)))).astype(bf16)
    up_low = (grad_hidden * silu).astype(bf16)
    gate_low, up_low = flow.tie((gate_low, up_low), (DOWN,), (QKV, OUT))
    flow.begin(GATE_UP, second, jnp.concatenate([gate_low, up_low], axis=1))
    grad_second = dot_nt(gate_low, w.gate) + dot_nt(up_low, w.up)
    grad_norm, gain_two = norm_back(middle, scale_two, w.gain_two, grad_second, features)
    grad_middle = grad + grad_norm
    grad_middle = flow.tie(grad_middle, (GATE_UP, DOWN) if early else (GATE_UP,), (QKV, OUT))
    middle_low = grad_middle.astype(bf16)
    flow.begin(OUT, attended, middle_low)
    grad_att = dot_nt(middle_low, w.out).astype(bf16)
    grad_att = dot_nt(grad_att, w.spread).astype(bf16)
    grad_att = flow.tie(grad_att, (OUT,) if early else (DOWN, OUT), ())
    grad_qkv = attend_back(turned_qk, values, grad_att, *tables, labels)
    grad_qkv = flow.tie(grad_qkv, (GATE_UP, OUT) if early else (GATE_UP, OUT, DOWN), (DOWN, QKV))
    grad_normed = dot_nt(grad_qkv, w.qkv)
    grad_norm, gain_one = norm_back(x, scale_one, w.gain_one, grad_normed, features)
    flow.begin(QKV, normed, (grad_qkv, gain_one, gain_two))
    grad = flow.tie(grad_middle + grad_norm, (QKV, GATE_UP), (GATE_UP,))
    flow.next_layer()
    return grad


class Weights:
    def __init__(self, **fields):
        self.__dict__.update(fields)


class Arriving:
    order = (
        ((0, 1, 0, 2, 0, 1, 0, 3, 1, 2, 0), (2, 3), (4, 1), (1, 3), (4, 5, 2), (2,)),
        ((4, 3, 3), (5,), (5, 4), (4,), (5,), (5,)),
    )

    def __init__(self, groups, unpack):
        self.groups = [(steps, next(steps)) for steps in groups]
        self.unpack = unpack

    def tie(self, value, turns):
        for index in turns:
            steps, waited = self.groups[index]
            value, got = lax.optimization_barrier((value, waited))
            try:
                self.groups[index] = (steps, steps.send(got))
            except StopIteration as end:
                self.groups[index] = (None, end.value)
        return value

    def weights(self, layer):
        return self.unpack([got for steps, got in self.groups[3 * layer : 3 * layer + 3] if steps is None])


class Flow:
    def __init__(self, begin, low):
        self.begun, self.low = begin, low
        self.now, self.before, self.done = {}, {}, []

    def begin(self, name, lhs, rhs):
        steps = self.begun(name, lhs, rhs, bool(self.before))
        self.now[name] = (steps, next(steps))

    def tie(self, value, now, before):
        tables = [(self.now, n) for n in now] + [(self.before, n) for n in before]
        tables = [(table, n) for table, n in tables if n in table and table[n][0] is not None]
        value, waited = lax.optimization_barrier((value, [table[n][1] for table, n in tables]))
        for (table, n), got in zip(tables, waited):
            self.advance(table, n, got)
        return value

    def advance(self, table, name, got):
        steps = table[name][0]
        try:
            table[name] = (steps, steps.send(got))
        except StopIteration as end:
            table[name] = (None, end.value)

    def next_layer(self):
        self.done.append(self.before)
        self.before, self.now = self.now, {}

    def finished(self):
        last, earlier = self.before, self.done[1:]
        self.tie((), (), (QKV, OUT))
        others = [table[name] for table in earlier for name in table] + [last[DOWN]]
        waited = self.tie([got for steps, got in others], (), (QKV,))
        for table in earlier:
            for name in table:
                table[name] = (table[name][0], waited.pop(0))
        last[DOWN] = (last[DOWN][0], waited.pop(0))
        self.tie((), (), (QKV, OUT, GATE_UP))
        for table in earlier + [last]:
            while any(steps is not None for steps, _ in table.values()):
                for name in table:
                    if table[name][0] is not None:
                        self.advance(table, name, table[name][1])
        return [{name: value for name, (_, value) in table.items()} for table in earlier + [last]]


class Halves:
    def __init__(self, n, features, hidden):
        self.n, self.features, self.hidden = n, features, hidden
        self.parts = 2 * n
        self.rows = features // self.parts
        self.padded = -(-self.rows // 16) * 16
        self.wide = self.parts * self.padded
        self.down_rows = hidden // self.parts
        self.section = lax.axis_index(SECTION)
        self.first = self.section == 0
        self.place = lax.axis_index(FSDP)
        lane = jnp.arange(self.wide, dtype=jnp.int32)
        inside = lane % self.padded
        natural = jnp.where(inside < self.rows, lane // self.padded * self.rows + inside, -1)
        self.spread = one_hot(features, natural)
        self.y = self.place // 2 % 2
        self.x = self.place % 2
        z, depth = self.place // 4, n // 4
        self.relative = self.block_order(lambda m: m)
        self.arrival = self.block_order(lambda m: (z - m + depth) % depth)

    def permuted_hidden(self, array):
        rows = array.shape[0]
        blocks = array.reshape(rows, self.parts, self.down_rows)
        cut = self.padded
        return jnp.concatenate(
            [
                blocks[:, :, :cut].reshape(rows, -1),
                blocks[:, :, cut : 2 * cut].reshape(rows, -1),
                blocks[:, :, 2 * cut :].reshape(rows, -1),
            ],
            axis=1,
        )

    def natural_hidden(self, array):
        rows = array.shape[0]
        cut = self.padded
        third = self.down_rows - 2 * cut
        one = array[:, : self.wide].reshape(rows, self.parts, cut)
        two = array[:, self.wide : 2 * self.wide].reshape(rows, self.parts, cut)
        three = array[:, 2 * self.wide :].reshape(rows, self.parts, third)
        return jnp.concatenate([one, two, three], axis=2).reshape(rows, self.hidden)

    def swap(self, array):
        return lax.ppermute(array, SECTION, [(0, 1), (1, 0)])

    def packed(self, weights):
        gain_one, query, key, value, out, gain_two, gate, up, down = weights
        self.wide_qkv = query.shape[1] + key.shape[1] + value.shape[1]
        self.cols_qkv = -(-(self.wide_qkv + 2) // 128) * 128
        spare = self.cols_qkv - self.wide_qkv - 2
        rows = query.shape[0]
        half = self.wide // 2

        def halves(parts):
            both = jnp.concatenate(parts, axis=1).reshape(2, self.rows, -1)
            return jnp.pad(both, ((0, 0), (0, self.padded - self.rows), (0, 0)))

        cut = self.padded
        carried = [self.carried(halves([
            query, key, value, gain_one[:, None], gain_two[:, None], jnp.zeros((rows, spare), bf16),
            dot(out, self.spread).astype(bf16),
        ]))]
        (gate, up, down), carried = lax.optimization_barrier(((gate, up, down), carried))
        carried.append(self.carried(halves([self.permuted_hidden(gate), self.permuted_hidden(up)])))
        down = dot(down, self.spread).astype(bf16).reshape(2, self.down_rows, self.wide)
        last = down[:, 2 * cut :]
        last = jnp.concatenate([last[:, :, :half], last[:, :, half:]], axis=1)
        carried.append(self.carried(jnp.concatenate([down[:, :cut], down[:, cut : 2 * cut], last], axis=2)))
        return [zero for zero, one in carried] + [one for zero, one in carried]

    def carried(self, halves):
        keep = jnp.where(self.first, halves[0], halves[1])
        got = self.swap(jnp.where(self.first, halves[1], halves[0]))
        return jnp.where(self.first, keep, got), jnp.where(self.first, got, keep)

    def source(self, weights):
        groups = [self.travelled(part) for part in self.packed(weights)]
        self.whole, self.left, self.right = self.order_matrices()

        whole, both = self.whole, self.wide

        def order(a):
            return dot(a, whole).astype(bf16)

        def order_hidden(a):
            last = a[:, 2 * both :]
            sides = [dot(last, self.left).astype(bf16), dot(last, self.right).astype(bf16)]
            return order(a[:, :both]), order(a[:, both : 2 * both]), jnp.concatenate(sides, axis=0)

        def unpack(groups):
            w = Weights(spread=self.spread, order=order, order_hidden=order_hidden)
            for unpacked, pieces in zip((self.attention, self.gate_up, self.down), groups):
                unpacked(w, pieces)
            return w

        return Arriving(groups, unpack)

    def assembled(self, pieces, shape, places):
        depth = self.n // 4
        part = self.padded
        count = len(places)

        def kernel(index, *refs):
            sources, out, held, came, gone = refs[: len(pieces)], *refs[len(pieces) :]
            arriving, leaving = [], []
            for number, source in enumerate(sources):
                arriving.append(pltpu.make_async_copy(source, held.at[number], came.at[number]))
                for m in range(depth):
                    block = number * depth + m
                    for place, (rows, columns, base, step, column) in enumerate(places):
                        leaving.append(
                            pltpu.make_async_copy(
                                held.at[
                                    number, pl.ds(m * part + rows[0], rows[1]), pl.ds(columns[0], columns[1])
                                ],
                                out.at[
                                    pl.ds(pl.multiple_of(base + index[block] * step, 16), rows[1]),
                                    pl.ds(column, columns[1]),
                                ],
                                gone.at[block * count + place],
                            )
                        )
            for copy in arriving:
                copy.start()
            for number, copy in enumerate(arriving):
                copy.wait()
                for sent in leaving[number * depth * count : (number + 1) * depth * count]:
                    sent.start()
            for copy in leaving:
                copy.wait()

        anywhere = pl.BlockSpec(memory_space=pl.ANY)
        return pl.pallas_call(
            kernel,
            out_shape=jax.ShapeDtypeStruct(shape, bf16),
            in_specs=[pl.BlockSpec(memory_space=pltpu.SMEM)] + [anywhere] * len(pieces),
            out_specs=anywhere,
            scratch_shapes=[
                pltpu.VMEM((len(pieces),) + pieces[0].shape, bf16),
                pltpu.SemaphoreType.DMA((len(pieces),)),
                pltpu.SemaphoreType.DMA((self.parts * count,)),
            ],
            compiler_params=pltpu.CompilerParams(vmem_limit_bytes=16 * 2**20),
            cost_estimate=pl.CostEstimate(flops=0, bytes_accessed=0, transcendentals=0),
        )(self.arrival, *pieces)

    def side_by_side(self, pieces):
        columns = pieces[0].shape[1]
        rows = self.padded
        return self.assembled(pieces, (self.wide, columns), [((0, rows), (0, columns), 0, rows, 0)])

    def attention(self, w, pieces):
        group = self.side_by_side(pieces)
        gains = group[:, self.wide_qkv : self.wide_qkv + 2].astype(f32).T
        w.gain_one, w.gain_two = gains[0], gains[1]
        w.qkv, w.out = group[:, : self.wide_qkv], group[:, self.cols_qkv :]

    def gate_up(self, w, pieces):
        group = self.side_by_side(pieces)
        w.gate, w.up = group[:, : self.hidden], group[:, self.hidden :]

    def down(self, w, pieces):
        wide, cut = self.wide, self.padded
        short, half = cut // 2, wide // 2
        w.down = self.assembled(
            pieces,
            (self.hidden, wide),
            [
                ((0, cut), (0, wide), 0, cut, 0),
                ((0, cut), (wide, wide), wide, cut, 0),
                ((0, short), (2 * wide, half), 2 * wide, short, 0),
                ((short, short), (2 * wide, half), 2 * wide, short, half),
            ],
        )

    def travelled(self, part):
        depth = self.n // 4
        part = yield part
        got = yield [
            lax.ppermute(part, FSDP, [(i, (i + 4 * k) % self.n) for i in range(self.n)])
            for k in range(1, depth)
        ]
        line = jnp.concatenate([part] + list(got), axis=0)
        first_route, second_route = self.routes()
        far = lax.ppermute(line, BOTH, first_route)
        across = [self.swap(line)]
        got = yield lax.ppermute(line, BOTH, second_route)
        across.append(self.swap(got))
        mine = [line, got]
        got = yield [far, lax.ppermute(got, BOTH, first_route)]
        across += [self.swap(one) for one in got]
        mine += got
        across = yield across
        return mine + across

    def block_order(self, chip_z):
        depth = self.n // 4
        block = jnp.arange(self.parts, dtype=jnp.int32)
        quarter = block // depth % 4
        core = self.section ^ (block // self.n)
        low, high = quarter % 2, quarter // 2
        other_x = jnp.where(core == 0, low, high)
        other_y = jnp.where(core == 0, high, low)
        chip = chip_z(block % depth) * 4 + (self.y ^ other_y) * 2 + (self.x ^ other_x)
        return chip * 2 + core

    def order_matrices(self):
        lane = jnp.arange(self.wide, dtype=jnp.int32)
        part = jnp.repeat(self.relative, self.padded)
        inside = lane % self.padded
        half = self.padded // 2
        block = part * half
        return (
            one_hot(self.wide, part * self.padded + inside),
            one_hot(self.wide // 2, jnp.where(inside < half, block + inside, -1)),
            one_hot(self.wide // 2, jnp.where(inside >= half, block + inside - half, -1)),
        )

    def routes(self):
        count = self.n

        def route(flips):
            return [
                (core * count + i, core * count + (i ^ flip))
                for core, flip in enumerate(flips)
                for i in range(count)
            ]

        return route((2, 1)), route((1, 2))

    def reduced(self, terms, direct=False):
        half = self.wide // 2

        def product(lo, hi):
            return jnp.concatenate([dot_tn(a[:, lo:hi], b) for a, b in terms], axis=1)

        first_route, second_route = self.routes()
        got = yield self.swap(product(half, self.wide).astype(bf16))
        mine = (product(0, half) + got.astype(f32)).astype(bf16)
        got = yield lax.ppermute(mine[half // 2 :], BOTH, first_route)
        mine = (mine[: half // 2].astype(f32) + got.astype(f32)).astype(bf16)
        got = yield lax.ppermute(mine[half // 4 :], BOTH, second_route)
        mine = (mine[: half // 4].astype(f32) + got.astype(f32)).astype(bf16)
        depth, part = self.n // 4, self.padded
        if direct:
            blocks = [
                lax.dynamic_slice_in_dim(mine, (self.place // 4 + k) % depth * part, part, 0)
                for k in range(depth)
            ]
            got = yield [
                lax.ppermute(blocks[k], FSDP, [(i, (i + 4 * k) % self.n) for i in range(self.n)])
                for k in range(1, depth)
            ]
            return sum((one.astype(f32) for one in got), blocks[0].astype(f32)).astype(bf16)
        lines = [[q + 4 * z for z in range(depth)] for q in range(4)]
        got = yield lax.psum_scatter(mine, FSDP, scatter_dimension=0, tiled=True, axis_index_groups=lines)
        return got

    def emitter(self):
        half = self.wide // 2

        def begin(name, lhs, rhs, last):
            if name == DOWN:
                one, two, both = lhs
                sides = jnp.concatenate([rhs[:, :half], rhs[:, half:]], axis=0)
                return self.reduced([(one, rhs), (two, rhs), (both, sides)])
            if name == GATE_UP:
                return self.reduced([(lhs, rhs)], direct=last)
            if name == OUT:
                return self.reduced([(lhs, rhs)], direct=True)
            grad_qkv, gain_one, gain_two = rhs
            length = lhs.shape[0]
            gains = jnp.pad(jnp.stack([gain_one, gain_two]), ((0, 14), (0, 0))).astype(bf16)
            ones = (jnp.arange(16)[:, None] == jnp.arange(self.cols_qkv)[None, :] - self.wide_qkv).astype(bf16)
            rhs = jnp.pad(grad_qkv, ((0, 0), (0, self.cols_qkv - self.wide_qkv)))
            rhs = jnp.concatenate([rhs, ones], axis=0)
            gains = dot(gains, self.whole).astype(bf16)
            return self.reduced([(jnp.concatenate([lhs, gains], axis=0), rhs)], direct=True)

        return begin

    def shares(self, sums):
        result = []
        for name in (DOWN, GATE_UP, OUT, QKV):
            zero, one = sums[0][name], sums[1][name]
            keep = jnp.where(self.first, zero, one)
            got = self.swap(jnp.where(self.first, one, zero))
            result.append(
                jnp.stack([jnp.where(self.first, keep, got), jnp.where(self.first, got, keep)]).astype(f32)
            )
        down, gate_up, out, qkv = result
        half = self.wide // 2
        cut = self.padded
        last = down[:, :, 2 * self.wide :]
        last = jnp.concatenate([last[:, : cut // 2], last[:, cut // 2 :]], axis=2)
        down = jnp.concatenate([down[:, :, : self.wide], down[:, :, self.wide : 2 * self.wide], last], axis=1)
        down = self.natural_features(down.reshape(2 * self.down_rows, self.wide))
        gate_up = gate_up[:, : self.rows].reshape(2 * self.rows, -1)
        out = self.natural_features(out[:, : self.rows].reshape(2 * self.rows, -1))
        qkv = qkv[:, : self.rows].reshape(2 * self.rows, -1)
        wide, narrow = HEADS * HD, KV * HD
        return (
            qkv[:, self.wide_qkv],
            qkv[:, :wide],
            qkv[:, wide : wide + narrow],
            qkv[:, wide + narrow : wide + 2 * narrow],
            out,
            qkv[:, self.wide_qkv + 1],
            self.natural_hidden(gate_up[:, : self.hidden]),
            self.natural_hidden(gate_up[:, self.hidden :]),
            down,
        )

    def natural_features(self, array):
        return dot_nt(array.astype(bf16), self.spread)


class Plain:
    def __init__(self, n, features, hidden):
        self.first = lax.axis_index(SECTION) == 0
        self.spread = one_hot(features, jnp.arange(features, dtype=jnp.int32))

    def source(self, weights):
        both = [lax.all_gather(part, (SECTION, FSDP), axis=0, tiled=True) for part in weights]
        both = [a.reshape((2, -1) + a.shape[1:]) for a in both]

        def same(a):
            return a

        def layer_of(layer):
            gain_one, query, key, value, out, gain_two, gate, up, down = [a[layer] for a in both]
            return Weights(
                gain_one=gain_one.astype(f32), gain_two=gain_two.astype(f32), out=out, gate=gate, up=up,
                down=down, qkv=jnp.concatenate([query, key, value], axis=1), spread=self.spread,
                order=same, order_hidden=same,
            )

        source = Arriving([], None)
        source.tie = lambda value, turns: value
        source.weights = layer_of
        return source

    def emitter(self):
        def reduced(a):
            part = lax.psum_scatter(a, FSDP, scatter_dimension=0, tiled=True)
            return lax.psum(part, SECTION)

        def begin(name, lhs, rhs, last):
            if name == QKV:
                grad_qkv, gain_one, gain_two = rhs
                yield ()
                return reduced(dot_tn(lhs, grad_qkv)), reduced(gain_one), reduced(gain_two)
            yield ()
            return reduced(dot_tn(lhs, rhs))

        return begin

    def shares(self, sums):
        own = jax.tree.map(lambda a, b: jnp.where(self.first, a, b), sums[0], sums[1])
        qkv, gain_one, gain_two = own[QKV]
        wide, narrow = HEADS * HD, KV * HD
        both = own[GATE_UP]
        hidden = both.shape[1] // 2
        return (
            gain_one,
            qkv[:, :wide],
            qkv[:, wide : wide + narrow],
            qkv[:, wide + narrow :],
            own[OUT],
            gain_two,
            both[:, :hidden],
            both[:, hidden:],
            own[DOWN],
        )


def on_device(inputs, cotangent, segments, positions, *weights):
    n = lax.axis_size(FSDP)
    features = inputs.shape[-1]
    hidden = weights[6].shape[-1]
    fits = n == 16 and features == 960 and hidden == 2560
    plan = (Halves if fits else Plain)(n, features, hidden)
    section = lax.axis_index(SECTION)
    first = section == 0
    source = plan.source([weight[0] for weight in weights])
    spread = plan.spread

    def mine(array):
        return lax.dynamic_index_in_dim(array, section, 0, keepdims=False)

    labels = mine(segments)
    tables = rope_tables(mine(positions))

    start = dot(mine(inputs), spread)
    grad = split_dot(mine(cotangent), spread)
    middle, weights_zero, kept_zero = forward(start, source, 0, labels, tables, features)
    flow = Flow(plan.emitter(), grad.astype(bf16))
    end, weights_one, kept_one = forward(middle, source, 1, labels, tables, features, flow)

    grad_middle = backward(middle, weights_one, labels, tables, features, kept_one, grad, flow)
    grad_start = backward(start, weights_zero, labels, tables, features, kept_zero, grad_middle, flow)
    sums_one, sums_zero = flow.finished()

    def exchanged(zero, one):
        keep = jnp.where(first, zero, one)
        sent = jnp.where(first, one, zero).astype(bf16)
        got = lax.ppermute(sent, SECTION, [(0, 1), (1, 0)])
        kept = keep.astype(bf16)
        rest = (keep - kept.astype(f32)).astype(bf16)
        kept = dot_nt(kept, spread) + dot_nt(rest, spread)
        got = dot_nt(got, spread)
        return jnp.stack([jnp.where(first, kept, got), jnp.where(first, got, kept)])[None]

    activations = exchanged(middle, end)
    input_grads = exchanged(grad_start, grad_middle)
    shares = plan.shares((sums_zero, sums_one))
    return (activations, input_grads) + tuple(share[None] for share in shares)


def solution(mesh):
    rows = P(SECTION, FSDP)
    matrix = P(SECTION, FSDP, None)
    weights = (rows, matrix, matrix, matrix, matrix, rows, matrix, matrix, matrix)
    tokens = P(None, FSDP, None)
    return jax.shard_map(
        on_device,
        mesh=mesh,
        in_specs=(tokens, tokens, P(None, FSDP), P(None, FSDP)) + weights,
        out_specs=(P(SECTION, None, FSDP, None), P(SECTION, None, FSDP, None)) + weights,
        check_vma=False,
    )
```

```python
import jax
import jax.numpy as jnp
from jax import lax
from jax.experimental import pallas as pl
from jax.experimental.pallas import tpu as pltpu
from jax.sharding import PartitionSpec as P

HEADS = 15
KV = 5
HD = 64
GROUP = HEADS // KV

SECTION = "section"
FSDP = "fsdp"
BOTH = (SECTION, FSDP)
QKV, OUT, GATE_UP, DOWN = range(4)

bf16 = jnp.bfloat16
f32 = jnp.float32
epsilon = 1e-05
rope_base = 100000.0


def dot(a, b):
    return jnp.dot(a, b, preferred_element_type=f32)


def dot_tn(a, b):
    return lax.dot_general(a, b, (((0,), (0,)), ((), ())), preferred_element_type=f32)


def dot_nt(a, b):
    return lax.dot_general(a, b, (((1,), (1,)), ((), ())), preferred_element_type=f32)


def one_hot(rows, targets):
    count = targets.shape[0]
    row = lax.broadcasted_iota(jnp.int32, (rows, count), 0)
    return (row == targets[None, :]).astype(bf16)


def split_dot(a, pick):
    high = a.astype(bf16)
    low = (a - high.astype(f32)).astype(bf16)
    return dot(high, pick) + dot(low, pick)


def rope_tables(places):
    half = HD // 2
    frequency = rope_base ** (-jnp.arange(half, dtype=f32) / half)
    angles = places.astype(f32)[:, None] * frequency
    cosine, sine = jnp.cos(angles), jnp.sin(angles)
    return jnp.concatenate([cosine] * 4, axis=1), jnp.concatenate([-sine, sine, -sine, sine], axis=1)


def norm_scale(v, features):
    return lax.rsqrt(jnp.sum(v * v, axis=-1, keepdims=True) / features + epsilon)


def norm_back(v, scale, gain, grad, features):
    gain_grad = jnp.sum(grad * v * scale, axis=0)
    weighted = grad * gain
    mean = jnp.sum(weighted * v, axis=-1, keepdims=True) / features
    return scale * weighted - v * (scale * scale * scale) * mean, gain_grad


ROWS = 128


def turned(block, cosine, sine):
    lane = lax.broadcasted_iota(jnp.int32, block.shape, 1)
    other = jnp.where(lane % HD < HD // 2, pltpu.roll(block, 128 - HD // 2, 1), pltpu.roll(block, HD // 2, 1))
    return block * cosine + other * sine


def fill_bias(bias, row_labels, column_labels):
    length = bias.shape[0]
    query = lax.broadcasted_iota(jnp.int32, (length, length), 0)
    key = lax.broadcasted_iota(jnp.int32, (length, length), 1)
    allowed = (row_labels[...] == column_labels[...]) & (query >= key)
    bias[...] = jnp.where(allowed, 0.0, -1e30)


def members(ref, start, rows, group):
    return jnp.concatenate(
        [ref[rows, (group * GROUP + j) * HD + start : (group * GROUP + j + 1) * HD + start] for j in range(GROUP)], axis=0
    )


def softmax(queries, keys, bias):
    scores = lax.dot_general(queries, keys, (((1,), (1,)), ((), ())), preferred_element_type=f32)
    scores = scores + jnp.concatenate([bias] * GROUP, axis=0)
    shifted = jnp.exp(scores - jnp.max(scores, axis=1, keepdims=True))
    return shifted / jnp.sum(shifted, axis=1, keepdims=True)


def attention_kernel(qkv, cosine, sine, row_labels, column_labels, attended, turned_qk, values, bias):
    length = qkv.shape[0]
    wide = HEADS * HD
    narrow = KV * HD
    fill_bias(bias, row_labels, column_labels)
    lane = lax.broadcasted_iota(jnp.int32, (length, 128), 1)
    for at in range(0, wide + narrow, 128):
        scale = jnp.where(lane + at < wide, HD ** -0.5, 1.0)
        block = turned(qkv[:, at : at + 128], cosine[...], sine[...])
        turned_qk[:, at : at + 128] = (block.astype(bf16).astype(f32) * scale).astype(bf16)
    values[...] = qkv[:, wide + narrow : wide + 2 * narrow].astype(bf16)
    for start in range(0, length, ROWS):
        rows = slice(start, start + ROWS)
        upto = slice(0, start + ROWS)
        heads = []
        for group in range(KV):
            queries = members(turned_qk, 0, rows, group)
            keys = turned_qk[upto, wide + group * HD : wide + (group + 1) * HD]
            probs = softmax(queries, keys, bias[rows, upto]).astype(bf16)
            mixed = jnp.dot(probs, values[upto, group * HD : (group + 1) * HD], preferred_element_type=f32)
            heads += [mixed[j * ROWS : (j + 1) * ROWS] for j in range(GROUP)]
        attended[rows, :] = jnp.concatenate(heads, axis=1).astype(bf16)


def attend(qkv, cosine, sine, labels):
    length = qkv.shape[0]
    wide, narrow = HEADS * HD, KV * HD
    return pl.pallas_call(
        attention_kernel,
        out_shape=[
            jax.ShapeDtypeStruct((length, wide), bf16),
            jax.ShapeDtypeStruct((length, wide + narrow), bf16),
            jax.ShapeDtypeStruct((length, narrow), bf16),
        ],
        scratch_shapes=[pltpu.VMEM((length, length), f32)],
        compiler_params=pltpu.CompilerParams(vmem_limit_bytes=32 * 2**20),
        cost_estimate=pl.CostEstimate(flops=0, bytes_accessed=0, transcendentals=0),
    )(qkv, cosine, sine, labels[:, None], labels[None, :])


def attention_back_kernel(turned_qk, values, grad_att, cosine, sine, row_labels, column_labels, grad_qkv, bias, grad_q, grad_v):
    length = turned_qk.shape[0]
    wide = HEADS * HD
    narrow = KV * HD
    fill_bias(bias, row_labels, column_labels)
    contract = (((0,), (0,)), ((), ()))
    for group in range(KV):
        total_k = [None] * (length // ROWS)
        total_v = [None] * (length // ROWS)
        for start in range(0, length, ROWS):
            rows = slice(start, start + ROWS)
            upto = slice(0, start + ROWS)
            queries = members(turned_qk, 0, rows, group)
            keys = turned_qk[upto, wide + group * HD : wide + (group + 1) * HD]
            mixed = values[upto, group * HD : (group + 1) * HD]
            grads = members(grad_att, 0, rows, group)
            probs = softmax(queries, keys, bias[rows, upto])
            grad_probs = lax.dot_general(grads, mixed, (((1,), (1,)), ((), ())), preferred_element_type=f32)
            part_v = lax.dot_general(probs.astype(bf16), grads, contract, preferred_element_type=f32)
            low = (probs * (grad_probs - jnp.sum(probs * grad_probs, axis=1, keepdims=True))).astype(bf16)
            part_k = lax.dot_general(low, queries, contract, preferred_element_type=f32)
            turned_back = jnp.dot(low, keys, preferred_element_type=f32) * HD ** -0.5
            for j in range(GROUP):
                head = group * GROUP + j
                grad_q[rows, head * HD : (head + 1) * HD] = turned_back[j * ROWS : (j + 1) * ROWS]
            for piece in range(start // ROWS + 1):
                inside = slice(piece * ROWS, (piece + 1) * ROWS)
                total_k[piece] = part_k[inside] if total_k[piece] is None else total_k[piece] + part_k[inside]
                total_v[piece] = part_v[inside] if total_v[piece] is None else total_v[piece] + part_v[inside]
        for piece in range(length // ROWS):
            inside = slice(piece * ROWS, (piece + 1) * ROWS)
            grad_q[inside, wide + group * HD : wide + (group + 1) * HD] = total_k[piece]
            grad_v[inside, group * HD : (group + 1) * HD] = total_v[piece]
    for at in range(0, wide + narrow, 128):
        grad_qkv[:, at : at + 128] = turned(grad_q[:, at : at + 128], cosine[...], -sine[...]).astype(bf16)
    grad_qkv[:, wide + narrow : wide + 2 * narrow] = grad_v[...].astype(bf16)


def attend_back(turned_qk, values, grad_att, cosine, sine, labels):
    length = turned_qk.shape[0]
    wide, narrow = HEADS * HD, KV * HD
    return pl.pallas_call(
        attention_back_kernel,
        out_shape=jax.ShapeDtypeStruct((length, wide + 2 * narrow), bf16),
        scratch_shapes=[pltpu.VMEM((length, length), f32), pltpu.VMEM((length, wide + narrow), f32), pltpu.VMEM((length, narrow), f32)],
        compiler_params=pltpu.CompilerParams(vmem_limit_bytes=32 * 2**20),
        cost_estimate=pl.CostEstimate(flops=0, bytes_accessed=0, transcendentals=0),
    )(turned_qk, values, grad_att, cosine, sine, labels[:, None], labels[None, :])


def forward(x, source, layer, labels, tables, features):
    turn = iter(source.order[layer])
    x = source.tie(x, next(turn))
    w = source.weights(layer)
    scale_one = norm_scale(x, features)
    normed = (x * scale_one * w.gain_one).astype(bf16)
    qkv = dot(normed, w.qkv)
    qkv = source.tie(qkv, next(turn))
    attended, turned_qk, values = attend(qkv, *tables, labels)
    attended = dot(attended, w.spread).astype(bf16)
    attended = source.tie(attended, next(turn))
    middle = x + dot(attended, w.out)
    middle = source.tie(middle, next(turn))
    w = source.weights(layer)
    scale_two = norm_scale(middle, features)
    second = (middle * scale_two * w.gain_two).astype(bf16)
    gate = dot(second, w.gate)
    up = dot(second, w.up)
    hidden = (jax.nn.silu(gate) * up).astype(bf16)
    hidden = source.tie(hidden, next(turn))
    w = source.weights(layer)
    output = middle + dot(hidden, w.down)
    return output, w, (
        scale_one, normed, turned_qk, values, attended, middle, scale_two, second, gate, up, hidden,
    )


def backward(x, w, labels, tables, features, kept, grad, flow):
    (scale_one, normed, turned_qk, values, attended, middle, scale_two, second, gate, up, hidden) = kept
    low = grad.astype(bf16)
    flow.begin(DOWN, hidden, low)
    grad_hidden = dot_nt(low, w.down)
    sig = jax.nn.sigmoid(gate)
    silu = gate * sig
    gate_low = (grad_hidden * up * (sig * (1.0 + gate * (1.0 - sig)))).astype(bf16)
    up_low = (grad_hidden * silu).astype(bf16)
    gate_low, up_low = flow.tie((gate_low, up_low), (DOWN,), (QKV, OUT))
    flow.begin(GATE_UP, second, jnp.concatenate([gate_low, up_low], axis=1))
    grad_second = dot_nt(gate_low, w.gate) + dot_nt(up_low, w.up)
    grad_norm, gain_two = norm_back(middle, scale_two, w.gain_two, grad_second, features)
    grad_middle = grad + grad_norm
    grad_middle = flow.tie(grad_middle, (GATE_UP,), (QKV, OUT))
    middle_low = grad_middle.astype(bf16)
    flow.begin(OUT, attended, middle_low)
    grad_att = dot_nt(middle_low, w.out).astype(bf16)
    grad_att = dot_nt(grad_att, w.spread).astype(bf16)
    grad_att = flow.tie(grad_att, (DOWN, OUT), ())
    grad_qkv = attend_back(turned_qk, values, grad_att, *tables, labels)
    grad_qkv = flow.tie(grad_qkv, (DOWN, GATE_UP), (DOWN, QKV))
    grad_normed = dot_nt(grad_qkv, w.qkv)
    grad_norm, gain_one = norm_back(x, scale_one, w.gain_one, grad_normed, features)
    flow.begin(QKV, normed, (grad_qkv, gain_one, gain_two))
    grad = flow.tie(grad_middle + grad_norm, (QKV, GATE_UP, OUT), (GATE_UP,))
    flow.next_layer()
    return grad


class Weights:
    def __init__(self, **fields):
        self.__dict__.update(fields)


class Arriving:
    order = (
        ((0, 1, 0, 2, 0, 1, 0, 3, 1, 2, 0), (2, 3), (4, 1), (1, 3), (4, 5, 2, 2)),
        ((4, 3, 3), (5,), (5, 4), (4,), (5, 5)),
    )

    def __init__(self, groups, unpack):
        self.groups = [(steps, next(steps)) for steps in groups]
        self.unpack = unpack

    def tie(self, value, turns):
        for index in turns:
            steps, waited = self.groups[index]
            value, got = lax.optimization_barrier((value, waited))
            try:
                self.groups[index] = (steps, steps.send(got))
            except StopIteration as end:
                self.groups[index] = (None, end.value)
        return value

    def weights(self, layer):
        return self.unpack([got for steps, got in self.groups[3 * layer : 3 * layer + 3] if steps is None])


class Flow:
    def __init__(self, begin):
        self.begun = begin
        self.now, self.before, self.done = {}, {}, []

    def begin(self, name, lhs, rhs):
        steps = self.begun(name, lhs, rhs)
        self.now[name] = (steps, next(steps))

    def tie(self, value, now, before):
        tables = [(self.now, n) for n in now] + [(self.before, n) for n in before]
        tables = [(table, n) for table, n in tables if n in table and table[n][0] is not None]
        value, waited = lax.optimization_barrier((value, [table[n][1] for table, n in tables]))
        for (table, n), got in zip(tables, waited):
            self.advance(table, n, got)
        return value

    def advance(self, table, name, got):
        steps = table[name][0]
        try:
            table[name] = (steps, steps.send(got))
        except StopIteration as end:
            table[name] = (None, end.value)

    def next_layer(self):
        self.done.append(self.before)
        self.before, self.now = self.now, {}

    def finished(self):
        last, earlier = self.before, self.done[1:]
        self.tie((), (), (QKV, OUT))
        others = [table[name] for table in earlier for name in table] + [last[DOWN]]
        waited = self.tie([got for steps, got in others], (), (QKV,))
        for table in earlier:
            for name in table:
                table[name] = (table[name][0], waited.pop(0))
        last[DOWN] = (last[DOWN][0], waited.pop(0))
        self.tie((), (), (QKV, OUT, GATE_UP))
        for table in earlier + [last]:
            while any(steps is not None for steps, _ in table.values()):
                for name in table:
                    if table[name][0] is not None:
                        self.advance(table, name, table[name][1])
        return [{name: value for name, (_, value) in table.items()} for table in earlier + [last]]


class Halves:
    def __init__(self, n, features, hidden):
        self.n, self.features, self.hidden = n, features, hidden
        self.parts = 2 * n
        self.rows = features // self.parts
        self.padded = -(-self.rows // 16) * 16
        self.wide = self.parts * self.padded
        self.down_rows = hidden // self.parts
        self.section = lax.axis_index(SECTION)
        self.first = self.section == 0
        self.place = lax.axis_index(FSDP)
        lane = jnp.arange(self.wide, dtype=jnp.int32)
        inside = lane % self.padded
        natural = jnp.where(inside < self.rows, lane // self.padded * self.rows + inside, -1)
        self.spread = one_hot(features, natural)
        self.y = self.place // 2 % 2
        self.x = self.place % 2
        z, depth = self.place // 4, n // 4
        self.relative = self.block_order(lambda m: m)
        self.arrival = self.block_order(lambda m: (z - m + depth) % depth)

    def permuted_hidden(self, array):
        rows = array.shape[0]
        blocks = array.reshape(rows, self.parts, self.down_rows)
        cut = self.padded
        return jnp.concatenate(
            [
                blocks[:, :, :cut].reshape(rows, -1),
                blocks[:, :, cut : 2 * cut].reshape(rows, -1),
                blocks[:, :, 2 * cut :].reshape(rows, -1),
            ],
            axis=1,
        )

    def natural_hidden(self, array):
        rows = array.shape[0]
        cut = self.padded
        third = self.down_rows - 2 * cut
        one = array[:, : self.wide].reshape(rows, self.parts, cut)
        two = array[:, self.wide : 2 * self.wide].reshape(rows, self.parts, cut)
        three = array[:, 2 * self.wide :].reshape(rows, self.parts, third)
        return jnp.concatenate([one, two, three], axis=2).reshape(rows, self.hidden)

    def swap(self, array):
        return lax.ppermute(array, SECTION, [(0, 1), (1, 0)])

    def packed(self, weights):
        gain_one, query, key, value, out, gain_two, gate, up, down = weights
        self.wide_qkv = query.shape[1] + key.shape[1] + value.shape[1]
        self.cols_qkv = -(-(self.wide_qkv + 2) // 128) * 128
        spare = self.cols_qkv - self.wide_qkv - 2
        rows = query.shape[0]
        half = self.wide // 2

        def halves(parts):
            both = jnp.concatenate(parts, axis=1).reshape(2, self.rows, -1)
            return jnp.pad(both, ((0, 0), (0, self.padded - self.rows), (0, 0)))

        cut = self.padded
        carried = [self.carried(halves([
            query, key, value, gain_one[:, None], gain_two[:, None], jnp.zeros((rows, spare), bf16),
            dot(out, self.spread).astype(bf16),
        ]))]
        (gate, up, down), carried = lax.optimization_barrier(((gate, up, down), carried))
        carried.append(self.carried(halves([self.permuted_hidden(gate), self.permuted_hidden(up)])))
        down = dot(down, self.spread).astype(bf16).reshape(2, self.down_rows, self.wide)
        last = down[:, 2 * cut :]
        last = jnp.concatenate([last[:, :, :half], last[:, :, half:]], axis=1)
        carried.append(self.carried(jnp.concatenate([down[:, :cut], down[:, cut : 2 * cut], last], axis=2)))
        return [zero for zero, one in carried] + [one for zero, one in carried]

    def carried(self, halves):
        keep = jnp.where(self.first, halves[0], halves[1])
        got = self.swap(jnp.where(self.first, halves[1], halves[0]))
        return jnp.where(self.first, keep, got), jnp.where(self.first, got, keep)

    def source(self, weights):
        groups = [self.travelled(part) for part in self.packed(weights)]
        self.whole, self.left, self.right = self.order_matrices()

        def unpack(groups):
            w = Weights(spread=self.spread)
            for unpacked, pieces in zip((self.attention, self.gate_up, self.down), groups):
                unpacked(w, pieces)
            return w

        return Arriving(groups, unpack)

    def assembled(self, pieces, shape, places):
        depth = self.n // 4
        part = self.padded
        count = len(places)

        def kernel(index, *refs):
            sources, out, held, came, gone = refs[: len(pieces)], *refs[len(pieces) :]
            arriving, leaving = [], []
            for number, source in enumerate(sources):
                arriving.append(pltpu.make_async_copy(source, held.at[number], came.at[number]))
                for m in range(depth):
                    block = number * depth + m
                    for place, (rows, columns, base, step, column) in enumerate(places):
                        leaving.append(
                            pltpu.make_async_copy(
                                held.at[
                                    number, pl.ds(m * part + rows[0], rows[1]), pl.ds(columns[0], columns[1])
                                ],
                                out.at[
                                    pl.ds(pl.multiple_of(base + index[block] * step, 16), rows[1]),
                                    pl.ds(column, columns[1]),
                                ],
                                gone.at[block * count + place],
                            )
                        )
            for copy in arriving:
                copy.start()
            for number, copy in enumerate(arriving):
                copy.wait()
                for sent in leaving[number * depth * count : (number + 1) * depth * count]:
                    sent.start()
            for copy in leaving:
                copy.wait()

        anywhere = pl.BlockSpec(memory_space=pl.ANY)
        return pl.pallas_call(
            kernel,
            out_shape=jax.ShapeDtypeStruct(shape, bf16),
            in_specs=[pl.BlockSpec(memory_space=pltpu.SMEM)] + [anywhere] * len(pieces),
            out_specs=anywhere,
            scratch_shapes=[
                pltpu.VMEM((len(pieces),) + pieces[0].shape, bf16),
                pltpu.SemaphoreType.DMA((len(pieces),)),
                pltpu.SemaphoreType.DMA((self.parts * count,)),
            ],
            compiler_params=pltpu.CompilerParams(vmem_limit_bytes=16 * 2**20),
            cost_estimate=pl.CostEstimate(flops=0, bytes_accessed=0, transcendentals=0),
        )(self.arrival, *pieces)

    def side_by_side(self, pieces):
        columns = pieces[0].shape[1]
        rows = self.padded
        return self.assembled(pieces, (self.wide, columns), [((0, rows), (0, columns), 0, rows, 0)])

    def attention(self, w, pieces):
        group = self.side_by_side(pieces)
        gains = group[:, self.wide_qkv : self.wide_qkv + 2].astype(f32).T
        w.gain_one, w.gain_two = gains[0], gains[1]
        w.qkv, w.out = group[:, : self.wide_qkv], group[:, self.cols_qkv :]

    def gate_up(self, w, pieces):
        group = self.side_by_side(pieces)
        w.gate, w.up = group[:, : self.hidden], group[:, self.hidden :]

    def down(self, w, pieces):
        wide, cut = self.wide, self.padded
        short, half = cut // 2, wide // 2
        w.down = self.assembled(
            pieces,
            (self.hidden, wide),
            [
                ((0, cut), (0, wide), 0, cut, 0),
                ((0, cut), (wide, wide), wide, cut, 0),
                ((0, short), (2 * wide, half), 2 * wide, short, 0),
                ((short, short), (2 * wide, half), 2 * wide, short, half),
            ],
        )

    def travelled(self, part):
        depth = self.n // 4
        part = yield part
        got = yield [
            lax.ppermute(part, FSDP, [(i, (i + 4 * k) % self.n) for i in range(self.n)])
            for k in range(1, depth)
        ]
        line = jnp.concatenate([part] + list(got), axis=0)
        first_route, second_route = self.routes()
        far = lax.ppermute(line, BOTH, first_route)
        across = [self.swap(line)]
        got = yield lax.ppermute(line, BOTH, second_route)
        across.append(self.swap(got))
        mine = [line, got]
        got = yield [far, lax.ppermute(got, BOTH, first_route)]
        across += [self.swap(one) for one in got]
        mine += got
        across = yield across
        return mine + across

    def block_order(self, chip_z):
        depth = self.n // 4
        block = jnp.arange(self.parts, dtype=jnp.int32)
        quarter = block // depth % 4
        core = self.section ^ (block // self.n)
        low, high = quarter % 2, quarter // 2
        other_x = jnp.where(core == 0, low, high)
        other_y = jnp.where(core == 0, high, low)
        chip = chip_z(block % depth) * 4 + (self.y ^ other_y) * 2 + (self.x ^ other_x)
        return chip * 2 + core

    def order_matrices(self):
        lane = jnp.arange(self.wide, dtype=jnp.int32)
        part = jnp.repeat(self.relative, self.padded)
        inside = lane % self.padded
        half = self.padded // 2
        block = part * half
        return (
            one_hot(self.wide, part * self.padded + inside),
            one_hot(self.wide // 2, jnp.where(inside < half, block + inside, -1)),
            one_hot(self.wide // 2, jnp.where(inside >= half, block + inside - half, -1)),
        )

    def routes(self):
        count = self.n

        def route(flips):
            return [
                (core * count + i, core * count + (i ^ flip))
                for core, flip in enumerate(flips)
                for i in range(count)
            ]

        return route((2, 1)), route((1, 2))

    def reduced(self, terms, direct=False):
        half = self.wide // 2

        def product(lo, hi):
            return jnp.concatenate([dot_tn(a[:, lo:hi], b) for a, b in terms], axis=1)

        first_route, second_route = self.routes()
        got = yield self.swap(product(half, self.wide).astype(bf16))
        mine = (product(0, half) + got.astype(f32)).astype(bf16)
        got = yield lax.ppermute(mine[half // 2 :], BOTH, first_route)
        mine = (mine[: half // 2].astype(f32) + got.astype(f32)).astype(bf16)
        got = yield lax.ppermute(mine[half // 4 :], BOTH, second_route)
        mine = (mine[: half // 4].astype(f32) + got.astype(f32)).astype(bf16)
        depth, part = self.n // 4, self.padded
        if direct:
            blocks = [
                lax.dynamic_slice_in_dim(mine, (self.place // 4 + k) % depth * part, part, 0)
                for k in range(depth)
            ]
            got = yield [
                lax.ppermute(blocks[k], FSDP, [(i, (i + 4 * k) % self.n) for i in range(self.n)])
                for k in range(1, depth)
            ]
            return sum((one.astype(f32) for one in got), blocks[0].astype(f32)).astype(bf16)
        lines = [[q + 4 * z for z in range(depth)] for q in range(4)]
        got = yield lax.psum_scatter(mine, FSDP, scatter_dimension=0, tiled=True, axis_index_groups=lines)
        return got

    def emitter(self):
        whole, half = self.whole, self.wide // 2

        def order(a):
            return dot(a, whole).astype(bf16)

        def begin(name, lhs, rhs):
            if name == DOWN:
                last = lhs[:, 2 * self.wide :]
                both = jnp.concatenate(
                    [dot(last, self.left).astype(bf16), dot(last, self.right).astype(bf16)], axis=0
                )
                sides = jnp.concatenate([rhs[:, :half], rhs[:, half:]], axis=0)
                terms = [
                    (order(lhs[:, : self.wide]), rhs),
                    (order(lhs[:, self.wide : 2 * self.wide]), rhs),
                    (both, sides),
                ]
                return self.reduced(terms)
            if name == GATE_UP:
                return self.reduced([(order(lhs), rhs)])
            if name == OUT:
                return self.reduced([(order(lhs), rhs)], direct=True)
            grad_qkv, gain_one, gain_two = rhs
            length = lhs.shape[0]
            gains = jnp.pad(jnp.stack([gain_one, gain_two]), ((0, 14), (0, 0))).astype(bf16)
            ones = (jnp.arange(16)[:, None] == jnp.arange(self.cols_qkv)[None, :] - self.wide_qkv).astype(bf16)
            rhs = jnp.pad(grad_qkv, ((0, 0), (0, self.cols_qkv - self.wide_qkv)))
            rhs = jnp.concatenate([rhs, ones], axis=0)
            return self.reduced([(order(jnp.concatenate([lhs, gains], axis=0)), rhs)], direct=True)

        return begin

    def shares(self, sums):
        result = []
        for name in (DOWN, GATE_UP, OUT, QKV):
            zero, one = sums[0][name], sums[1][name]
            keep = jnp.where(self.first, zero, one)
            got = self.swap(jnp.where(self.first, one, zero))
            result.append(
                jnp.stack([jnp.where(self.first, keep, got), jnp.where(self.first, got, keep)]).astype(f32)
            )
        down, gate_up, out, qkv = result
        half = self.wide // 2
        cut = self.padded
        last = down[:, :, 2 * self.wide :]
        last = jnp.concatenate([last[:, : cut // 2], last[:, cut // 2 :]], axis=2)
        down = jnp.concatenate([down[:, :, : self.wide], down[:, :, self.wide : 2 * self.wide], last], axis=1)
        down = self.natural_features(down.reshape(2 * self.down_rows, self.wide))
        gate_up = gate_up[:, : self.rows].reshape(2 * self.rows, -1)
        out = self.natural_features(out[:, : self.rows].reshape(2 * self.rows, -1))
        qkv = qkv[:, : self.rows].reshape(2 * self.rows, -1)
        wide, narrow = HEADS * HD, KV * HD
        return (
            qkv[:, self.wide_qkv],
            qkv[:, :wide],
            qkv[:, wide : wide + narrow],
            qkv[:, wide + narrow : wide + 2 * narrow],
            out,
            qkv[:, self.wide_qkv + 1],
            self.natural_hidden(gate_up[:, : self.hidden]),
            self.natural_hidden(gate_up[:, self.hidden :]),
            down,
        )

    def natural_features(self, array):
        return dot_nt(array.astype(bf16), self.spread)


class Plain:
    def __init__(self, n, features, hidden):
        self.first = lax.axis_index(SECTION) == 0
        self.spread = one_hot(features, jnp.arange(features, dtype=jnp.int32))

    def source(self, weights):
        both = [lax.all_gather(part, (SECTION, FSDP), axis=0, tiled=True) for part in weights]
        both = [a.reshape((2, -1) + a.shape[1:]) for a in both]

        def layer_of(layer):
            gain_one, query, key, value, out, gain_two, gate, up, down = [a[layer] for a in both]
            return Weights(
                gain_one=gain_one.astype(f32), gain_two=gain_two.astype(f32), out=out, gate=gate, up=up,
                down=down, qkv=jnp.concatenate([query, key, value], axis=1), spread=self.spread,
            )

        source = Arriving([], None)
        source.tie = lambda value, turns: value
        source.weights = layer_of
        return source

    def emitter(self):
        def reduced(a):
            part = lax.psum_scatter(a, FSDP, scatter_dimension=0, tiled=True)
            return lax.psum(part, SECTION)

        def begin(name, lhs, rhs):
            if name == QKV:
                grad_qkv, gain_one, gain_two = rhs
                yield ()
                return reduced(dot_tn(lhs, grad_qkv)), reduced(gain_one), reduced(gain_two)
            yield ()
            return reduced(dot_tn(lhs, rhs))

        return begin

    def shares(self, sums):
        own = jax.tree.map(lambda a, b: jnp.where(self.first, a, b), sums[0], sums[1])
        qkv, gain_one, gain_two = own[QKV]
        wide, narrow = HEADS * HD, KV * HD
        both = own[GATE_UP]
        hidden = both.shape[1] // 2
        return (
            gain_one,
            qkv[:, :wide],
            qkv[:, wide : wide + narrow],
            qkv[:, wide + narrow :],
            own[OUT],
            gain_two,
            both[:, :hidden],
            both[:, hidden:],
            own[DOWN],
        )


def on_device(inputs, cotangent, segments, positions, *weights):
    n = lax.axis_size(FSDP)
    features = inputs.shape[-1]
    hidden = weights[6].shape[-1]
    fits = n == 16 and features == 960 and hidden == 2560
    plan = (Halves if fits else Plain)(n, features, hidden)
    section = lax.axis_index(SECTION)
    first = section == 0
    source = plan.source([weight[0] for weight in weights])
    spread = plan.spread

    def mine(array):
        return lax.dynamic_index_in_dim(array, section, 0, keepdims=False)

    labels = mine(segments)
    tables = rope_tables(mine(positions))

    start = dot(mine(inputs), spread)
    middle, weights_zero, kept_zero = forward(start, source, 0, labels, tables, features)
    end, weights_one, kept_one = forward(middle, source, 1, labels, tables, features)

    grad = split_dot(mine(cotangent), spread)
    flow = Flow(plan.emitter())
    grad_middle = backward(middle, weights_one, labels, tables, features, kept_one, grad, flow)
    grad_start = backward(start, weights_zero, labels, tables, features, kept_zero, grad_middle, flow)
    sums_one, sums_zero = flow.finished()

    def exchanged(zero, one):
        keep = jnp.where(first, zero, one)
        sent = jnp.where(first, one, zero).astype(bf16)
        got = lax.ppermute(sent, SECTION, [(0, 1), (1, 0)])
        kept = keep.astype(bf16)
        rest = (keep - kept.astype(f32)).astype(bf16)
        kept = dot_nt(kept, spread) + dot_nt(rest, spread)
        got = dot_nt(got, spread)
        return jnp.stack([jnp.where(first, kept, got), jnp.where(first, got, kept)])[None]

    activations = exchanged(middle, end)
    input_grads = exchanged(grad_start, grad_middle)
    shares = plan.shares((sums_zero, sums_one))
    return (activations, input_grads) + tuple(share[None] for share in shares)


def solution(mesh):
    rows = P(SECTION, FSDP)
    matrix = P(SECTION, FSDP, None)
    weights = (rows, matrix, matrix, matrix, matrix, rows, matrix, matrix, matrix)
    tokens = P(None, FSDP, None)
    return jax.shard_map(
        on_device,
        mesh=mesh,
        in_specs=(tokens, tokens, P(None, FSDP), P(None, FSDP)) + weights,
        out_specs=(P(SECTION, None, FSDP, None), P(SECTION, None, FSDP, None)) + weights,
        check_vma=False,
    )
```
